32 devices in a mesh: wide: 16 (over z, y, core), narrow: 2 (over x).
Axes of the slice: x: 2, y: 2, z: 4, core: 2. Of those that a mesh axis runs over, the one named last changes fastest.
Arguments:
- tokens: bfloat16 [2048, 2048], P('wide', 'narrow'), may hold values from -6 to 6
- expert_ids: int32 [2048, 6], P('wide'), may hold values from 0 to 15, all different within a row; in each aligned block of 128 rows (0 to 127, 128 to 255, ...) at most 56 rows name the same one
- route_weights: bfloat16 [2048, 6], P('wide'), may hold values from 0.049804688 to 0.5
- w_gate: bfloat16 [16, 1408, 2048], P('wide', 'narrow'), may hold values from -0.125 to 0.125
- w_up: bfloat16 [16, 1408, 2048], P('wide', 'narrow'), may hold values from -0.125 to 0.125
- w_down: bfloat16 [16, 1408, 2048], P('wide', 'narrow'), may hold values from -0.15625 to 0.15625
Outputs:
- mixed: bfloat16 [2048, 2048], P('wide', 'narrow')
The draws below stay inside these ranges and needn't reach their ends.
Inputs may be any that keep to these rules, and one draw needn't show every extreme that they name: `expert_ids`: within a row the 6 experts differ. Among the 128 tokens of one aligned block, no expert is named more than 56 times, a bound that some block reaches.
All inputs are finite; a program needn't handle non-finite values.
Results may differ from the reference program's by a relative error of at most 0.017.
Values may be sent and summed in bfloat16 or wider, within the bound.
No kernel may reach another device: no remote copies, remote signals or barrier semaphores. Data moves between devices by JAX's collectives and lax.ppermute only.
A program may use at most 64 MiB of HBM per device.

```python
import math
import jax
import jax.numpy as jnp
import numpy as np
from jax import lax

D = 2048
FF = 1408
TOP = 6
TOK_DEV = 128
TOKENS = 2048
EXPERTS = 16
CAP = 56
N_NARROW = 2


def block_scale(stream_key, shape, pieces, smallest, top_value):
    level, own = 1.0, jax.random.fold_in(stream_key, 6)
    for dim, parts in pieces:
        heights = jnp.exp(jax.random.uniform(jax.random.fold_in(own, dim), (parts,), jnp.float32, smallest / len(pieces), top_value / len(pieces)))
        level = level * jnp.repeat(heights, shape[dim] // parts).reshape([-1 if axis == dim else 1 for axis in range(len(shape))])
    return level


def assign_block(own_key, own, number, rows, count, top, most, skew):
    ranking = jax.random.permutation(own_key, count)
    crowded, common = load_shares(count, rows * top, most, skew, True), load_shares(count, rows * top, most, skew, False)
    places = jnp.arange(count)

    def named(tallies, offset_by):
        used = int((tallies > 0).sum())
        fixed = max(1, used // 4)
        moved = fixed + (places - fixed + offset_by * (used - fixed)) % max(1, count - fixed)
        return jnp.zeros((count,), jnp.int32).at[ranking[jnp.where(places < fixed, places, moved)]].set(jnp.asarray(tallies, jnp.int32))

    tallies = jnp.where(number % 4 == 0, named(crowded, number // 4), named(common, number - number // 4 - 1))
    mixed = jax.random.permutation(jax.random.fold_in(own, 3), count)
    source_of, sink = mixed[0:count // 2 * 2:2], mixed[1:count // 2 * 2:2]
    margin = jnp.minimum(tallies[source_of] - 1, most - tallies[sink]) // 2
    margin = jnp.where((source_of == ranking[0]) | (sink == ranking[0]) | (tallies[sink] == 0), 0, jnp.maximum(margin, 0))
    moved = jax.random.randint(jax.random.fold_in(own, 4), (count // 2,), 0, 1 << 20) % (margin + 1)
    tallies = tallies.at[source_of].add(-moved).at[sink].add(moved)
    labels = jnp.searchsorted(jnp.cumsum(tallies), jnp.arange(rows * top), side="right").astype(jnp.int32)
    grid = labels.reshape(top, rows).T
    grid = grid[jax.random.permutation(jax.random.fold_in(own, 1), rows)]
    offset_by = jax.random.randint(jax.random.fold_in(own, 2), (rows, 1), 0, top)
    return jnp.take_along_axis(grid, (jnp.arange(top)[None, :] + offset_by) % top, axis=1)


def load_shares(count, total, most, lean, full):
    portions = [(1 << 20) // math.isqrt(rank ** lean) + 1 for rank in range(1, count + 1)]
    largest = most if full else min(most, max(-(-total // count), total * portions[0] // sum(portions)))
    least = 1 if total - largest >= count - 1 else 0
    counts, surplus = [largest] + [least] * (count - 1), total - largest - least * (count - 1)
    while surplus > 0:
        movable = [i for i in range(1, count) if counts[i] < largest] or [i for i in range(1, count) if counts[i] < most]
        mass, left = sum([portions[i] for i in movable]), surplus
        for i in movable:
            extra = min(most - counts[i], max(1, left * portions[i] // mass), surplus)
            counts[i] = counts[i] + extra
            surplus = surplus - extra
    return np.array(counts)


def noise(key, shape, deviation, limit, pieces=(), kind=jnp.bfloat16):
    array = deviation * jax.random.normal(key, shape, jnp.float32)
    if pieces:
        array = array * block_scale(key, shape, pieces, -0.22, 0.18)
    return jnp.clip(array, -limit, limit).astype(kind)


def setup_inputs(seed: int = 0) -> dict:
    seeds = jax.random.split(jax.random.key(seed), 7)
    tokens = noise(seeds[0], (TOKENS, D), 1.0, 6.0, ((0, 16), (1, 2)))
    expert_ids_keys = jax.random.split(jax.random.fold_in(seeds[1], 1), TOKENS // TOK_DEV)
    expert_ids_turns = jax.random.permutation(jax.random.fold_in(seeds[1], 3), TOKENS // TOK_DEV)
    expert_ids = jax.vmap(lambda own, number: assign_block(jax.random.fold_in(seeds[1], 2), own, number, TOK_DEV, EXPERTS, TOP, CAP, 2))(expert_ids_keys, expert_ids_turns).reshape((TOKENS, TOP))
    route_weights = jnp.clip(0.049804688 + 0.4501953 * jax.random.uniform(seeds[2], (TOKENS, TOP), jnp.float32) ** block_scale(seeds[2], (TOKENS, TOP), ((0, 16),), -0.2, 0.2), 0.049804688, 0.5).astype(jnp.bfloat16)
    w_gate = noise(seeds[3], (EXPERTS, FF, D), D ** -0.5, 0.125, ((0, 16), (1, 2)))
    w_up = noise(seeds[4], (EXPERTS, FF, D), D ** -0.5, 0.125, ((0, 16), (1, 2)))
    w_down = noise(seeds[5], (EXPERTS, FF, D), FF ** -0.5, 0.15625, ((0, 16), (1, 2)))
    return dict(tokens=tokens, expert_ids=expert_ids, route_weights=route_weights, w_gate=w_gate, w_up=w_up, w_down=w_down)


def reference(tokens, expert_ids, route_weights, w_gate, w_up, w_down):
    blocks = TOKENS // TOK_DEV
    pairs = TOK_DEV * TOP
    block_ids = expert_ids.reshape(blocks, pairs)
    onehot = (block_ids[:, :, None] == jnp.arange(EXPERTS, dtype=jnp.int32)[None, None, :]).astype(jnp.int32)
    running = jnp.cumsum(onehot, axis=1)
    slot_index = jnp.sum(running * onehot, axis=2) - 1
    block_num = jnp.arange(blocks, dtype=jnp.int32)[:, None]
    row_index = (block_num * CAP + slot_index).reshape(-1).astype(jnp.int32)
    token_index = (block_num * TOK_DEV + jnp.arange(pairs, dtype=jnp.int32)[None, :] // TOP).reshape(-1).astype(jnp.int32)
    flat_ids = block_ids.reshape(-1).astype(jnp.int32)
    row_token = jnp.full((EXPERTS, blocks * CAP), TOKENS, dtype=jnp.int32)
    row_token = row_token.at[flat_ids, row_index].set(token_index)
    row_weight = jnp.zeros((EXPERTS, blocks * CAP), dtype=jnp.float32)
    row_weight = row_weight.at[flat_ids, row_index].set(route_weights.reshape(-1).astype(jnp.float32))
    padded = jnp.concatenate([tokens, jnp.zeros((1, D), dtype=tokens.dtype)], axis=0)
    group_ff = FF // N_NARROW

    def one_expert(total, inputs):
        gate_e, up_e, down_e, tok_e, weight_e = inputs
        slot_rows = padded[tok_e]
        gate_proj = jnp.dot(slot_rows, gate_e.T, preferred_element_type=jnp.float32)
        up_proj = jnp.dot(slot_rows, up_e.T, preferred_element_type=jnp.float32)
        hidden = (jax.nn.silu(gate_proj) * up_proj).astype(jnp.bfloat16)
        hidden = lax.optimization_barrier(hidden)
        partial_value = jnp.einsum("rgf,gfd->rgd", hidden.reshape(-1, N_NARROW, group_ff).astype(jnp.float32),
                             down_e.reshape(N_NARROW, group_ff, D).astype(jnp.float32)).astype(jnp.bfloat16)
        partial_value = lax.optimization_barrier(partial_value)
        expert_out = jnp.sum(partial_value.astype(jnp.float32), axis=1)
        total = total.at[tok_e].add(weight_e[:, None] * expert_out)
        return total, None

    start = jnp.zeros((TOKENS + 1, D), dtype=jnp.float32)
    total, unused = lax.scan(one_expert, start, (w_gate, w_up, w_down, row_token, row_weight))
    return total[:TOKENS].astype(jnp.bfloat16)
```

```python
import functools

import jax
import jax.numpy as jnp
from jax import lax
from jax.experimental import pallas as pl
from jax.experimental.pallas import tpu as pltpu
from jax.sharding import PartitionSpec as P

CORE, Y, NEAR, FAR = 1, 2, 4, 8
VMEM_BYTES = 48 << 20
F32, BF16 = jnp.float32, jnp.bfloat16


def general(tokens, expert_ids, route_weights, w_gate, w_up, w_down):
    tok_rows = expert_ids.shape[0]
    top_count = expert_ids.shape[1]
    local_experts = w_gate.shape[0]
    groups_wide = lax.axis_size("wide")
    experts_all = local_experts * groups_wide
    capacity = 7 * tok_rows * top_count // (6 * experts_all)
    slots_all = experts_all * capacity
    width = w_down.shape[2]
    flat_ids = expert_ids.reshape(-1)
    onehot = (flat_ids[:, None] == jnp.arange(experts_all, dtype=jnp.int32)[None, :]).astype(
        jnp.int32
    )
    running = jnp.cumsum(onehot, axis=0)
    slot_index = jnp.sum(running * onehot, axis=1) - 1
    destination = (flat_ids * capacity + slot_index).reshape(tok_rows, top_count)
    slot_table = (
        destination[:, :, None] == jnp.arange(slots_all, dtype=jnp.int32)[None, None, :]
    ).astype(jnp.float32)
    dispatch = jnp.sum(slot_table, axis=1).astype(jnp.bfloat16)
    whole = lax.all_gather(tokens, "narrow", axis=1, tiled=True)
    outgoing = jnp.einsum("ts,td->sd", dispatch, whole, preferred_element_type=jnp.float32).astype(
        jnp.bfloat16
    )
    received = lax.all_to_all(outgoing, "wide", split_axis=0, concat_axis=0, tiled=True)
    slot_rows = received.reshape(groups_wide, local_experts, capacity, width)
    gate_proj = jnp.einsum("secd,efd->secf", slot_rows, w_gate, preferred_element_type=jnp.float32)
    up_proj = jnp.einsum("secd,efd->secf", slot_rows, w_up, preferred_element_type=jnp.float32)
    hidden = (jax.nn.silu(gate_proj) * up_proj).astype(jnp.bfloat16)
    partial_value = jnp.einsum(
        "secf,efd->secd", hidden, w_down, preferred_element_type=jnp.float32
    ).astype(jnp.bfloat16)
    partial_value = partial_value.reshape(slots_all, width)
    summed = lax.psum_scatter(partial_value, "narrow", scatter_dimension=1, tiled=True).astype(
        jnp.float32
    )
    returned = lax.all_to_all(
        summed.astype(jnp.bfloat16), "wide", split_axis=0, concat_axis=0, tiled=True
    ).astype(summed.dtype)
    picked = returned[destination.reshape(-1)].reshape(tok_rows, top_count, -1)
    mixed = jnp.sum(route_weights.astype(jnp.float32)[:, :, None] * picked, axis=1)
    return mixed.astype(jnp.bfloat16)


def kernel_call(body, out_shape, n_in, flops, bytes_accessed, scratch=()):
    vmem = pl.BlockSpec(memory_space=pltpu.VMEM)
    return pl.pallas_call(
        body,
        out_shape=out_shape,
        in_specs=[pl.BlockSpec(memory_space=pltpu.SMEM)] + [vmem] * n_in,
        out_specs=jax.tree.map(lambda _: vmem, out_shape),
        scratch_shapes=list(scratch),
        compiler_params=pltpu.CompilerParams(vmem_limit_bytes=VMEM_BYTES),
        cost_estimate=pl.CostEstimate(flops=flops, bytes_accessed=bytes_accessed, transcendentals=0),
    )


def pair_rows(place_ref, routing_ref, dz, capacity, weighted):
    me = place_ref[0]
    toks = routing_ref.shape[2]
    before = lax.broadcasted_iota(jnp.int32, (toks, toks), 0) <= lax.broadcasted_iota(
        jnp.int32, (toks, toks), 1
    )
    rows = []
    for expert in (me, me ^ CORE):
        for block in (me ^ (NEAR * dz), me ^ (NEAR * dz + Y)):
            rows.append(routing_ref[block, pl.ds(expert, 1), :])
    weight = jnp.concatenate(rows, axis=0)
    chosen = weight > 0
    count = jnp.dot(
        jnp.where(chosen, 1.0, 0.0).astype(BF16),
        jnp.where(before, 1.0, 0.0).astype(BF16),
        preferred_element_type=F32,
    )
    slot = jnp.where(chosen, count.astype(jnp.int32) - 1, -1)
    tables = []
    for expert in (0, 1):
        first, second = slot[2 * expert : 2 * expert + 1], slot[2 * expert + 1 : 2 * expert + 2]
        second = jnp.where(second >= 0, second + capacity, -1)
        at = jnp.concatenate([first, second], axis=1)
        value = jnp.concatenate(
            [weight[2 * expert : 2 * expert + 1], weight[2 * expert + 1 : 2 * expert + 2]], axis=1
        )
        here = lax.broadcasted_iota(jnp.int32, (2 * capacity, 2 * toks), 0) == at
        tables.append(jnp.where(here, value if weighted else 1.0, 0.0))
    return jnp.concatenate(tables, axis=0).astype(BF16)


def dispatch_kernel(capacity, dz_list, place_ref, routing_ref, *refs):
    units, (own_ref, send_ref) = refs[:-2], refs[-2:]
    rows, half = 2 * capacity, own_ref.shape[1] // 2
    for p, dz in enumerate(dz_list):
        table = pair_rows(place_ref, routing_ref, dz, capacity, False)
        for dx in (0, 1):
            first, second = units[4 * p + dx], units[4 * p + 2 + dx]
            block = jnp.concatenate([first[...], second[...]], axis=0)
            out = jnp.dot(table, block, preferred_element_type=F32).astype(BF16)
            own_ref[p * rows : (p + 1) * rows, dx * half : (dx + 1) * half] = out[:rows]
            send_ref[p * rows : (p + 1) * rows, dx * half : (dx + 1) * half] = out[rows:]


def dispatch(place, routing, units, dz_list, capacity):
    half = units[0].shape[1]
    shape = jax.ShapeDtypeStruct((2 * capacity * len(dz_list), 2 * half), BF16)
    flops = len(dz_list) * 2 * 4 * capacity * 256 * 2 * half
    return kernel_call(
        functools.partial(dispatch_kernel, capacity, dz_list),
        (shape, shape),
        1 + len(units),
        flops,
        len(units) * 256 * 1024 * 2,
    )(place, routing, *units)


def ffn_kernel(place_ref, own_ref, other_ref, gate_ref, up_ref, down_ref, own_out, other_out, rows_ref, hidden_ref):
    x = place_ref[1]
    n = own_ref.shape[0]
    half = own_ref.shape[1] // 2
    ff = gate_ref.shape[1]
    rows_ref[:n] = own_ref[...]
    rows_ref[n:] = other_ref[...]
    mine = pl.ds(pl.multiple_of(x * half, half), half)
    theirs = pl.ds(pl.multiple_of((1 - x) * half, half), half)
    step = 256
    nt = (((1,), (1,)), ((), ()))
    for low in range(0, ff, step):
        high = min(low + step, ff)

        def project(ref):
            return lax.dot_general(
                rows_ref[:, :half], ref[0, low:high, mine], nt, preferred_element_type=F32
            ) + lax.dot_general(
                rows_ref[:, half:], ref[0, low:high, theirs], nt, preferred_element_type=F32
            )

        gate = project(gate_ref)
        up = project(up_ref)
        hidden_ref[:, low:high] = (gate / (1.0 + jnp.exp(-gate)) * up).astype(BF16)
    for j, columns in enumerate((mine, theirs)):
        out = jnp.dot(hidden_ref[...], down_ref[0, :, columns], preferred_element_type=F32).astype(BF16)
        own_out[:, j * half : (j + 1) * half] = out[:n]
        other_out[:, j * half : (j + 1) * half] = out[n:]


def ffn(place, own, other, w_gate, w_up, w_down):
    n, width = own.shape
    ff = w_gate.shape[1]
    shape = jax.ShapeDtypeStruct((n, width), BF16)
    return kernel_call(
        ffn_kernel,
        (shape, shape),
        5,
        6 * 2 * n * width * ff,
        6 * width * ff + 8 * n * width,
        scratch=(pltpu.VMEM((2 * n, width), BF16), pltpu.VMEM((2 * n, ff), BF16)),
    )(place, own, other, w_gate, w_up, w_down)


def combine_kernel(capacity, dz_list, place_ref, routing_ref, own_ref, other_ref, *outs):
    rows, half = 2 * capacity, own_ref.shape[1] // 2
    toks = routing_ref.shape[2]
    for p, dz in enumerate(dz_list):
        table = pair_rows(place_ref, routing_ref, dz, capacity, True)
        keep, send = outs[2 * p], outs[2 * p + 1]
        for dx in (0, 1):
            columns = slice(dx * half, (dx + 1) * half)
            value = jnp.concatenate(
                [own_ref[p * rows : (p + 1) * rows, columns], other_ref[p * rows : (p + 1) * rows, columns]],
                axis=0,
            )
            out = lax.dot_general(
                table, value, (((0,), (0,)), ((), ())), preferred_element_type=F32
            ).astype(BF16)
            for dy in (0, 1):
                block = out[dy * toks : (dy + 1) * toks]
                if p % 2 == 0:
                    (send if dy else keep)[dx] = block
                else:
                    (send if dx else keep)[dy] = block


def combine(place, routing, own, other, dz_list, capacity):
    toks, half = routing.shape[2], own.shape[1] // 2
    shape = jax.ShapeDtypeStruct((2, toks, half), BF16)
    return kernel_call(
        functools.partial(combine_kernel, capacity, dz_list),
        (shape,) * (2 * len(dz_list)),
        3,
        len(dz_list) * 2 * 4 * capacity * 256 * 2 * half,
        len(dz_list) * 8 * toks * half * 2,
    )(place, routing, own, other)


def local(tokens, expert_ids, route_weights, w_gate, w_up, w_down):
    wide = lax.axis_size("wide")
    tok_rows, top_count = expert_ids.shape
    capacity = 7 * tok_rows * top_count // (6 * wide)
    me, x = lax.axis_index("wide"), lax.axis_index("narrow")
    place = jnp.stack([me, x]).astype(jnp.int32)

    def hop(value, bit):
        return lax.ppermute(value, "wide", [(i, i ^ bit) for i in range(wide)])

    def hop_x(value):
        return lax.ppermute(value, "narrow", [(0, 1), (1, 0)])

    def add(a, b):
        return (a.astype(F32) + b.astype(F32)).astype(BF16)

    named = expert_ids.T[:, None, :] == jnp.arange(wide, dtype=jnp.int32)[None, :, None]
    routing = jnp.sum(jnp.where(named, route_weights.astype(F32).T[:, None, :], 0.0), axis=0)
    routing = lax.all_gather(routing, "wide", axis=0, tiled=False)

    column = [tokens, hop(tokens, NEAR), hop(tokens, FAR), None]
    column[3] = hop(column[2], NEAR)

    def gather(dz):
        unit = column[dz]
        if dz % 2 == 0:
            beside = hop_x(unit)
            far = hop(jnp.stack([unit, beside]), Y)
            return [unit, beside, far[0], far[1]]
        beside = hop(unit, Y)
        far = hop_x(jnp.stack([unit, beside]))
        return [unit, far[0], beside, far[1]]

    def chunk(dz_list):
        units = [unit for dz in dz_list for unit in gather(dz)]
        own, send = dispatch(place, routing, units, dz_list, capacity)
        other = hop(send, CORE)
        own, other = ffn(place, own, other, w_gate, w_up, w_down)
        other = hop(other, CORE)
        keep_a, send_a, keep_b, send_b = combine(place, routing, own, other, dz_list, capacity)
        sum_a = add(keep_a, hop(send_a, Y))
        sum_b = add(keep_b, hop_x(send_b))
        return add(sum_a[0], hop_x(sum_a[1])), add(sum_b[0], hop(sum_b[1], Y))

    mine, near = chunk((0, 1))
    far, both = chunk((2, 3))
    near = hop(near, NEAR)
    far = add(far, hop(both, NEAR))
    far = hop(far, FAR)
    return (mine.astype(F32) + near.astype(F32) + far.astype(F32)).astype(BF16)


def solution(mesh):
    in_specs = (
        P("wide", "narrow"),
        P("wide", None),
        P("wide", None),
        P("wide", "narrow", None),
        P("wide", "narrow", None),
        P("wide", "narrow", None),
    )
    out_specs = P("wide", "narrow")
    fits = mesh.shape["wide"] == 16 and mesh.shape["narrow"] == 2
    return jax.shard_map(
        local if fits else general, mesh=mesh, in_specs=in_specs, out_specs=out_specs, check_vma=False
    )
```

```python
import functools

import jax
import jax.numpy as jnp
from jax import lax
from jax.experimental import pallas as pl
from jax.experimental.pallas import tpu as pltpu
from jax.sharding import PartitionSpec as P

CORE, Y, NEAR, FAR = 1, 2, 4, 8
VMEM_BYTES = 20 << 20
F32, BF16 = jnp.float32, jnp.bfloat16


def general(tokens, expert_ids, route_weights, w_gate, w_up, w_down):
    tok_rows = expert_ids.shape[0]
    top_count = expert_ids.shape[1]
    local_experts = w_gate.shape[0]
    groups_wide = lax.axis_size("wide")
    experts_all = local_experts * groups_wide
    capacity = 7 * tok_rows * top_count // (6 * experts_all)
    slots_all = experts_all * capacity
    width = w_down.shape[2]
    flat_ids = expert_ids.reshape(-1)
    onehot = (flat_ids[:, None] == jnp.arange(experts_all, dtype=jnp.int32)[None, :]).astype(
        jnp.int32
    )
    running = jnp.cumsum(onehot, axis=0)
    slot_index = jnp.sum(running * onehot, axis=1) - 1
    destination = (flat_ids * capacity + slot_index).reshape(tok_rows, top_count)
    slot_table = (
        destination[:, :, None] == jnp.arange(slots_all, dtype=jnp.int32)[None, None, :]
    ).astype(jnp.float32)
    dispatch = jnp.sum(slot_table, axis=1).astype(jnp.bfloat16)
    whole = lax.all_gather(tokens, "narrow", axis=1, tiled=True)
    outgoing = jnp.einsum("ts,td->sd", dispatch, whole, preferred_element_type=jnp.float32).astype(
        jnp.bfloat16
    )
    received = lax.all_to_all(outgoing, "wide", split_axis=0, concat_axis=0, tiled=True)
    slot_rows = received.reshape(groups_wide, local_experts, capacity, width)
    gate_proj = jnp.einsum("secd,efd->secf", slot_rows, w_gate, preferred_element_type=jnp.float32)
    up_proj = jnp.einsum("secd,efd->secf", slot_rows, w_up, preferred_element_type=jnp.float32)
    hidden = (jax.nn.silu(gate_proj) * up_proj).astype(jnp.bfloat16)
    partial_value = jnp.einsum(
        "secf,efd->secd", hidden, w_down, preferred_element_type=jnp.float32
    ).astype(jnp.bfloat16)
    partial_value = partial_value.reshape(slots_all, width)
    summed = lax.psum_scatter(partial_value, "narrow", scatter_dimension=1, tiled=True).astype(
        jnp.float32
    )
    returned = lax.all_to_all(
        summed.astype(jnp.bfloat16), "wide", split_axis=0, concat_axis=0, tiled=True
    ).astype(summed.dtype)
    picked = returned[destination.reshape(-1)].reshape(tok_rows, top_count, -1)
    mixed = jnp.sum(route_weights.astype(jnp.float32)[:, :, None] * picked, axis=1)
    return mixed.astype(jnp.bfloat16)


def kernel_call(body, out_shape, n_in, flops, bytes_accessed, scratch=()):
    vmem = pl.BlockSpec(memory_space=pltpu.VMEM)
    return pl.pallas_call(
        body,
        out_shape=out_shape,
        in_specs=[pl.BlockSpec(memory_space=pltpu.SMEM)] + [vmem] * n_in,
        out_specs=jax.tree.map(lambda _: vmem, out_shape),
        scratch_shapes=list(scratch),
        compiler_params=pltpu.CompilerParams(vmem_limit_bytes=VMEM_BYTES),
        cost_estimate=pl.CostEstimate(flops=flops, bytes_accessed=bytes_accessed, transcendentals=0),
    )


def pair_rows(place_ref, routing_ref, dz, capacity, weighted):
    me = place_ref[0]
    toks = routing_ref.shape[2]
    before = lax.broadcasted_iota(jnp.int32, (toks, toks), 0) <= lax.broadcasted_iota(
        jnp.int32, (toks, toks), 1
    )
    rows = []
    for expert in (me, me ^ CORE):
        for dy in (0, 1):
            rows.append(routing_ref[2 * dz + dy, pl.ds(expert, 1), :])
    weight = jnp.concatenate(rows, axis=0)
    chosen = weight > 0
    count = jnp.dot(
        jnp.where(chosen, 1.0, 0.0).astype(BF16),
        jnp.where(before, 1.0, 0.0).astype(BF16),
        preferred_element_type=F32,
    )
    slot = jnp.where(chosen, count.astype(jnp.int32) - 1, -1)
    tables = []
    for expert in (0, 1):
        first, second = slot[2 * expert : 2 * expert + 1], slot[2 * expert + 1 : 2 * expert + 2]
        second = jnp.where(second >= 0, second + capacity, -1)
        at = jnp.concatenate([first, second], axis=1)
        value = jnp.concatenate(
            [weight[2 * expert : 2 * expert + 1], weight[2 * expert + 1 : 2 * expert + 2]], axis=1
        )
        here = lax.broadcasted_iota(jnp.int32, (2 * capacity, 2 * toks), 0) == at
        tables.append(jnp.where(here, value if weighted else 1.0, 0.0))
    return jnp.concatenate(tables, axis=0).astype(BF16)


def dispatch_kernel(capacity, dz_list, place_ref, routing_ref, *refs):
    units, (own_ref, send_ref) = refs[:-2], refs[-2:]
    rows, half = 2 * capacity, own_ref.shape[1] // 2
    for p, dz in enumerate(dz_list):
        table = pair_rows(place_ref, routing_ref, dz, capacity, False)
        for dx in (0, 1):
            first, second = units[4 * p + dx], units[4 * p + 2 + dx]
            block = jnp.concatenate([first[...], second[...]], axis=0)
            out = jnp.dot(table, block, preferred_element_type=F32).astype(BF16)
            own_ref[p * rows : (p + 1) * rows, dx * half : (dx + 1) * half] = out[:rows]
            send_ref[p * rows : (p + 1) * rows, dx * half : (dx + 1) * half] = out[rows:]


def dispatch(place, routing, units, dz_list, capacity):
    half = units[0].shape[1]
    shape = jax.ShapeDtypeStruct((2 * capacity * len(dz_list), 2 * half), BF16)
    flops = len(dz_list) * 2 * 4 * capacity * 256 * 2 * half
    return kernel_call(
        functools.partial(dispatch_kernel, capacity, dz_list),
        (shape, shape),
        1 + len(units),
        flops,
        len(units) * 256 * 1024 * 2,
    )(place, routing, *units)


def ffn_kernel(place_ref, own_ref, other_ref, gate_ref, up_ref, down_ref, own_out, other_out, rows_ref, hidden_ref):
    x = place_ref[1]
    n = own_ref.shape[0]
    half = own_ref.shape[1] // 2
    ff = gate_ref.shape[1]
    rows_ref[:n] = own_ref[...]
    rows_ref[n:] = other_ref[...]
    mine = pl.ds(pl.multiple_of(x * half, half), half)
    theirs = pl.ds(pl.multiple_of((1 - x) * half, half), half)
    step = 256
    nt = (((1,), (1,)), ((), ()))
    for low in range(0, ff, step):
        high = min(low + step, ff)

        def project(ref):
            return lax.dot_general(
                rows_ref[:, :half], ref[0, low:high, mine], nt, preferred_element_type=F32
            ) + lax.dot_general(
                rows_ref[:, half:], ref[0, low:high, theirs], nt, preferred_element_type=F32
            )

        gate = project(gate_ref)
        up = project(up_ref)
        hidden_ref[:, low:high] = (gate / (1.0 + jnp.exp(-gate)) * up).astype(BF16)
    for j, columns in enumerate((mine, theirs)):
        out = jnp.dot(hidden_ref[...], down_ref[0, :, columns], preferred_element_type=F32).astype(BF16)
        own_out[:, j * half : (j + 1) * half] = out[:n]
        other_out[:, j * half : (j + 1) * half] = out[n:]


def ffn(place, own, other, w_gate, w_up, w_down):
    n, width = own.shape
    ff = w_gate.shape[1]
    shape = jax.ShapeDtypeStruct((n, width), BF16)
    return kernel_call(
        ffn_kernel,
        (shape, shape),
        5,
        6 * 2 * n * width * ff,
        6 * width * ff + 8 * n * width,
        scratch=(pltpu.VMEM((2 * n, width), BF16), pltpu.VMEM((2 * n, ff), BF16)),
    )(place, own, other, w_gate, w_up, w_down)


def combine_kernel(capacity, dz_list, place_ref, routing_ref, own_ref, other_ref, *outs):
    rows, half = 2 * capacity, own_ref.shape[1] // 2
    toks = routing_ref.shape[2]
    for p, dz in enumerate(dz_list):
        table = pair_rows(place_ref, routing_ref, dz, capacity, True)
        keep, send = outs[2 * p], outs[2 * p + 1]
        for dx in (0, 1):
            columns = slice(dx * half, (dx + 1) * half)
            value = jnp.concatenate(
                [own_ref[p * rows : (p + 1) * rows, columns], other_ref[p * rows : (p + 1) * rows, columns]],
                axis=0,
            )
            out = lax.dot_general(
                table, value, (((0,), (0,)), ((), ())), preferred_element_type=F32
            ).astype(BF16)
            for dy in (0, 1):
                block = out[dy * toks : (dy + 1) * toks]
                if p % 2 == 0:
                    (send if dy else keep)[dx] = block
                else:
                    (send if dx else keep)[dy] = block


def combine(place, routing, own, other, dz_list, capacity):
    toks, half = routing.shape[2], own.shape[1] // 2
    shape = jax.ShapeDtypeStruct((2, toks, half), BF16)
    return kernel_call(
        functools.partial(combine_kernel, capacity, dz_list),
        (shape,) * (2 * len(dz_list)),
        3,
        len(dz_list) * 2 * 4 * capacity * 256 * 2 * half,
        len(dz_list) * 8 * toks * half * 2,
    )(place, routing, own, other)


def local(tokens, expert_ids, route_weights, w_gate, w_up, w_down):
    wide = lax.axis_size("wide")
    tok_rows, top_count = expert_ids.shape
    capacity = 7 * tok_rows * top_count // (6 * wide)
    me, x = lax.axis_index("wide"), lax.axis_index("narrow")
    place = jnp.stack([me, x]).astype(jnp.int32)

    def hop(value, bit):
        return lax.ppermute(value, "wide", [(i, i ^ bit) for i in range(wide)])

    def hop_x(value):
        return lax.ppermute(value, "narrow", [(0, 1), (1, 0)])

    def add(a, b):
        return (a.astype(F32) + b.astype(F32)).astype(BF16)

    named = expert_ids.T[:, None, :] == jnp.arange(wide, dtype=jnp.int32)[None, :, None]
    routing = jnp.sum(jnp.where(named, route_weights.astype(F32).T[:, None, :], 0.0), axis=0)
    routing = jnp.stack([routing, hop(routing, Y)])
    routing = jnp.concatenate([routing, hop(routing, NEAR)])
    routing = jnp.concatenate([routing, hop(routing, FAR)])

    column = [tokens, hop(tokens, NEAR), hop(tokens, FAR), None]
    column[3] = hop(column[2], NEAR)

    def gather(dz):
        unit = column[dz]
        if dz % 2 == 0:
            beside = hop_x(unit)
            far = hop(jnp.stack([unit, beside]), Y)
            return [unit, beside, far[0], far[1]]
        beside = hop(unit, Y)
        far = hop_x(jnp.stack([unit, beside]))
        return [unit, far[0], beside, far[1]]

    def chunk(dz_list):
        units = [unit for dz in dz_list for unit in gather(dz)]
        own, send = dispatch(place, routing, units, dz_list, capacity)
        other = hop(send, CORE)
        own, other = ffn(place, own, other, w_gate, w_up, w_down)
        other = hop(other, CORE)
        keep_a, send_a, keep_b, send_b = combine(place, routing, own, other, dz_list, capacity)
        sum_a = add(keep_a, hop(send_a, Y))
        sum_b = add(keep_b, hop_x(send_b))
        return add(sum_a[0], hop_x(sum_a[1])), add(sum_b[0], hop(sum_b[1], Y))

    mine, near = chunk((0, 1))
    far, both = chunk((2, 3))
    near = hop(near, NEAR)
    far = add(far, hop(both, NEAR))
    far = hop(far, FAR)
    return (mine.astype(F32) + near.astype(F32) + far.astype(F32)).astype(BF16)


def solution(mesh):
    in_specs = (
        P("wide", "narrow"),
        P("wide", None),
        P("wide", None),
        P("wide", "narrow", None),
        P("wide", "narrow", None),
        P("wide", "narrow", None),
    )
    out_specs = P("wide", "narrow")
    fits = mesh.shape["wide"] == 16 and mesh.shape["narrow"] == 2
    return jax.shard_map(
        local if fits else general, mesh=mesh, in_specs=in_specs, out_specs=out_specs, check_vma=False
    )
```

```python
import functools

import jax
import jax.numpy as jnp
from jax import lax
from jax.experimental import pallas as pl
from jax.experimental.pallas import tpu as pltpu
from jax.sharding import PartitionSpec as P

CORE, Y, NEAR, FAR = 1, 2, 4, 8
VMEM_BYTES = 20 << 20
ROUTE_FLOPS = 40_000_000_000
PACK_FLOPS = 10_000_000_000
MIX_FLOPS = 0
FIRST_X = ("0",)
ORDER = ["u1p", "gather2", "pack0", "gather2b", "gather1", "expert0", "u3p", "u3_xy", "gather3", "pack2", "u1_x", "gather1b", "mix0", "expert2", "mix2", "u3_yx", "u1_ys", "pack3", "pack1", "sum0", "expert31", "sum2", "mix31", "out2", "end2", "sum31", "out0", "out31"]
F32, BF16 = jnp.float32, jnp.bfloat16


def general(tokens, expert_ids, route_weights, w_gate, w_up, w_down):
    tok_rows = expert_ids.shape[0]
    top_count = expert_ids.shape[1]
    local_experts = w_gate.shape[0]
    groups_wide = lax.axis_size("wide")
    experts_all = local_experts * groups_wide
    capacity = 7 * tok_rows * top_count // (6 * experts_all)
    slots_all = experts_all * capacity
    width = w_down.shape[2]
    flat_ids = expert_ids.reshape(-1)
    onehot = (flat_ids[:, None] == jnp.arange(experts_all, dtype=jnp.int32)[None, :]).astype(
        jnp.int32
    )
    running = jnp.cumsum(onehot, axis=0)
    slot_index = jnp.sum(running * onehot, axis=1) - 1
    destination = (flat_ids * capacity + slot_index).reshape(tok_rows, top_count)
    slot_table = (
        destination[:, :, None] == jnp.arange(slots_all, dtype=jnp.int32)[None, None, :]
    ).astype(jnp.float32)
    dispatch = jnp.sum(slot_table, axis=1).astype(jnp.bfloat16)
    whole = lax.all_gather(tokens, "narrow", axis=1, tiled=True)
    outgoing = jnp.einsum("ts,td->sd", dispatch, whole, preferred_element_type=jnp.float32).astype(
        jnp.bfloat16
    )
    received = lax.all_to_all(outgoing, "wide", split_axis=0, concat_axis=0, tiled=True)
    slot_rows = received.reshape(groups_wide, local_experts, capacity, width)
    gate_proj = jnp.einsum("secd,efd->secf", slot_rows, w_gate, preferred_element_type=jnp.float32)
    up_proj = jnp.einsum("secd,efd->secf", slot_rows, w_up, preferred_element_type=jnp.float32)
    hidden = (jax.nn.silu(gate_proj) * up_proj).astype(jnp.bfloat16)
    partial_value = jnp.einsum(
        "secf,efd->secd", hidden, w_down, preferred_element_type=jnp.float32
    ).astype(jnp.bfloat16)
    partial_value = partial_value.reshape(slots_all, width)
    summed = lax.psum_scatter(partial_value, "narrow", scatter_dimension=1, tiled=True).astype(
        jnp.float32
    )
    returned = lax.all_to_all(
        summed.astype(jnp.bfloat16), "wide", split_axis=0, concat_axis=0, tiled=True
    ).astype(summed.dtype)
    picked = returned[destination.reshape(-1)].reshape(tok_rows, top_count, -1)
    mixed = jnp.sum(route_weights.astype(jnp.float32)[:, :, None] * picked, axis=1)
    return mixed.astype(jnp.bfloat16)


def kernel_call(body, out_shape, n_in, flops, bytes_accessed, scratch=()):
    vmem = pl.BlockSpec(memory_space=pltpu.VMEM)
    return pl.pallas_call(
        body,
        out_shape=out_shape,
        in_specs=[pl.BlockSpec(memory_space=pltpu.SMEM)] + [vmem] * n_in,
        out_specs=jax.tree.map(lambda _: vmem, out_shape),
        scratch_shapes=list(scratch),
        compiler_params=pltpu.CompilerParams(vmem_limit_bytes=VMEM_BYTES),
        cost_estimate=pl.CostEstimate(flops=flops, bytes_accessed=bytes_accessed, transcendentals=0),
    )


def route_kernel(ids_ref, weights_ref, tokens_ref, out_ref):
    toks = tokens_ref.shape[0]
    experts = out_ref.shape[0] - toks
    total = jnp.zeros((experts, toks), F32)
    number = lax.broadcasted_iota(jnp.int32, (experts, toks), 0)
    weights = weights_ref[...].astype(F32)
    for k in range(ids_ref.shape[0]):
        total += jnp.where(number == ids_ref[k : k + 1, :], weights[k : k + 1, :], 0.0)
    out_ref[:toks] = tokens_ref[...]
    out_ref[toks:] = jnp.zeros((experts, out_ref.shape[1]), BF16)
    out_ref[toks:, :toks] = total.astype(BF16)


def route(ids, weights, tokens, experts):
    vmem = pl.BlockSpec(memory_space=pltpu.VMEM)
    return pl.pallas_call(
        route_kernel,
        out_shape=jax.ShapeDtypeStruct((tokens.shape[0] + experts, tokens.shape[1]), BF16),
        in_specs=[vmem] * 3,
        out_specs=vmem,
        cost_estimate=pl.CostEstimate(flops=ROUTE_FLOPS, bytes_accessed=1 << 16, transcendentals=0),
    )(ids, weights, tokens)


def routing_table(routes, toks, capacity, weighted):
    me = lax.axis_index("wide")
    before = lax.broadcasted_iota(jnp.int32, (toks, toks), 0) <= lax.broadcasted_iota(
        jnp.int32, (toks, toks), 1
    )
    number = lax.broadcasted_iota(jnp.int32, routes[0].shape, 0)
    weight = jnp.concatenate(
        [
            jnp.sum(jnp.where(number == expert, block, 0.0), axis=0, keepdims=True)
            for expert in (me, me ^ CORE)
            for block in routes
        ],
        axis=0,
    )
    chosen = weight > 0
    count = jnp.dot(
        jnp.where(chosen, 1.0, 0.0).astype(BF16),
        jnp.where(before, 1.0, 0.0).astype(BF16),
        preferred_element_type=F32,
    )
    slot = jnp.where(chosen, count.astype(jnp.int32) - 1, -1)
    tables = []
    for expert in (0, 1):
        first, second = slot[2 * expert : 2 * expert + 1], slot[2 * expert + 1 : 2 * expert + 2]
        second = jnp.where(second >= 0, second + capacity, -1)
        at = jnp.concatenate([first, second], axis=1)
        value = jnp.concatenate(
            [weight[2 * expert : 2 * expert + 1], weight[2 * expert + 1 : 2 * expert + 2]], axis=1
        )
        here = lax.broadcasted_iota(jnp.int32, (2 * capacity, 2 * toks), 0) == at
        tables.append(jnp.where(here, value if weighted else 1.0, 0.0))
    return jnp.concatenate(tables, axis=0).astype(BF16)


def dispatch_kernel(capacity, toks, layout, routes, place_ref, *refs):
    units, (own_ref, send_ref, routes_ref) = refs[:-3], refs[-3:]
    rows, half = 2 * capacity, own_ref.shape[1] // 2
    experts = routes_ref.shape[1]
    blocks = [units[number][row : row + experts, :toks].astype(F32) for number, row in routes]
    for i, block in enumerate(blocks):
        routes_ref[i] = block
    table = routing_table(blocks, toks, capacity, False)
    for dx in (0, 1):
        parts = []
        for number, at, count, column, dy, row in sorted(layout, key=lambda part: part[4:]):
            if column == dx:
                parts.append(units[number][at : at + count])
        out = jnp.dot(table, jnp.concatenate(parts, axis=0), preferred_element_type=F32).astype(BF16)
        own_ref[:, dx * half : (dx + 1) * half] = out[:rows]
        send_ref[:, dx * half : (dx + 1) * half] = out[rows:]


def dispatch(place, units, layout, routes, capacity, toks, experts):
    half = units[0].shape[-1]
    shape = jax.ShapeDtypeStruct((2 * capacity, 2 * half), BF16)
    return kernel_call(
        functools.partial(dispatch_kernel, capacity, toks, layout, routes),
        (shape, shape, jax.ShapeDtypeStruct((2, experts, toks), F32)),
        len(units),
        PACK_FLOPS if len(units) == 4 else 0,
        0,
    )(place, *units)


def ffn_kernel(count, place_ref, *refs):
    inputs, (gate_ref, up_ref, down_ref) = refs[:count], refs[count : count + 3]
    outputs, (rows_ref, hidden_ref) = refs[count + 3 : -2], refs[-2:]
    x = place_ref[1]
    n, half = inputs[0].shape[0], inputs[0].shape[1] // 2
    ff = gate_ref.shape[1]
    for i, ref in enumerate(inputs):
        rows_ref[i * n : (i + 1) * n] = ref[...]
    mine = pl.ds(pl.multiple_of(x * half, half), half)
    theirs = pl.ds(pl.multiple_of((1 - x) * half, half), half)
    step = 256
    nt = (((1,), (1,)), ((), ()))
    for low in range(0, ff, step):
        high = min(low + step, ff)

        def project(ref):
            return lax.dot_general(
                rows_ref[:, :half], ref[0, low:high, mine], nt, preferred_element_type=F32
            ) + lax.dot_general(
                rows_ref[:, half:], ref[0, low:high, theirs], nt, preferred_element_type=F32
            )

        gate = project(gate_ref)
        up = project(up_ref)
        hidden_ref[:, low:high] = (gate / (1.0 + jnp.exp(-gate)) * up).astype(BF16)
    for j, columns in enumerate((mine, theirs)):
        out = jnp.dot(hidden_ref[...], down_ref[0, :, columns], preferred_element_type=F32).astype(BF16)
        for i, ref in enumerate(outputs):
            ref[:, j * half : (j + 1) * half] = out[i * n : (i + 1) * n]


def ffn(place, inputs, w_gate, w_up, w_down):
    count = len(inputs)
    n, width = inputs[0].shape
    ff = w_gate.shape[1]
    return kernel_call(
        functools.partial(ffn_kernel, count),
        (jax.ShapeDtypeStruct((n, width), BF16),) * count,
        count + 3,
        count * n * width * ff,
        0,
        scratch=(pltpu.VMEM((count * n, width), BF16), pltpu.VMEM((count * n, ff), BF16)),
    )(place, *inputs, w_gate, w_up, w_down)


def combine_kernel(capacity, layouts, place_ref, *refs):
    count = len(layouts)
    inputs, outs = refs[: 3 * count], refs[3 * count :]
    half = inputs[1].shape[1] // 2
    toks = inputs[0].shape[2]
    for p, layout in enumerate(layouts):
        routes_ref, own_ref, other_ref = inputs[3 * p : 3 * p + 3]
        table = routing_table([routes_ref[0], routes_ref[1]], toks, capacity, True)
        for dx in (0, 1):
            columns = slice(dx * half, (dx + 1) * half)
            value = jnp.concatenate([own_ref[:, columns], other_ref[:, columns]], axis=0)
            out = lax.dot_general(
                table, value, (((0,), (0,)), ((), ())), preferred_element_type=F32
            ).astype(BF16)
            for number, at, count, column, dy, row in layout:
                if column == dx:
                    low = dy * toks + row
                    outs[number][at : at + count] = out[low : low + count]


def combine(place, pairs, layouts, capacity):
    toks, half = pairs[0][0].shape[2], pairs[0][1].shape[1] // 2
    parts = [part for layout in layouts for part in layout]
    rows = [0] * (1 + max(part[0] for part in parts))
    for part in parts:
        rows[part[0]] += part[2]
    return kernel_call(
        functools.partial(combine_kernel, capacity, layouts),
        tuple(jax.ShapeDtypeStruct((count, half), BF16) for count in rows),
        3 * len(pairs),
        MIX_FLOPS,
        0,
    )(place, *[array for pair in pairs for array in pair])


def local(tokens, expert_ids, route_weights, w_gate, w_up, w_down):
    wide = lax.axis_size("wide")
    tok_rows, top_count = expert_ids.shape
    capacity = 7 * tok_rows * top_count // (6 * wide)
    cut, full = tok_rows // 2, tok_rows
    me, x = lax.axis_index("wide"), lax.axis_index("narrow")
    place = jnp.stack([me, x]).astype(jnp.int32)

    def hop(value, bit):
        return lax.ppermute(value, "wide", [(i, i ^ bit) for i in range(wide)])

    def hop_x(value):
        return lax.ppermute(value, "narrow", [(0, 1), (1, 0)])

    def hop_xy(value):
        pairs = [(2 * i + j, 2 * (i ^ Y) + 1 - j) for i in range(wide) for j in (0, 1)]
        return lax.ppermute(value, ("wide", "narrow"), pairs)

    def add(a, b):
        return (a.astype(F32) + b.astype(F32)).astype(BF16)

    def rows(*parts):
        return jnp.concatenate(parts, axis=0)

    held, last = {}, []

    def take(*names):
        values = [held[name] for name in names]
        tied = lax.optimization_barrier(tuple(values + last))
        for name, value in zip(names, tied):
            held[name] = value
        last[:] = [tied[0]]
        return tied[0] if len(names) == 1 else tied[: len(names)]

    def put(**values):
        held.update(values)
        last[:] = [next(iter(values.values()))]

    halves = (
        (0, 0, full, 0, 0, 0),
        (1, 0, cut, 1, 0, 0),
        (2, 0, cut, 0, 1, cut),
        (3, 0, cut, 0, 1, 0),
        (3, cut, cut, 1, 1, 0),
        (4, 0, cut, 1, 0, cut),
        (4, cut, cut, 1, 1, cut),
    )
    by_dy = ((0, 0, full, 0, 0, 0), (0, full, full, 1, 0, 0), (1, 0, full, 0, 1, 0), (1, full, full, 1, 1, 0))
    by_dx = ((0, 0, full, 0, 0, 0), (0, full, full, 0, 1, 0), (1, 0, full, 1, 0, 0), (1, full, full, 1, 1, 0))
    by_half = (
        (0, 0, cut, 0, 0, 0),
        (0, cut, cut, 1, 0, 0),
        (1, 0, cut, 0, 1, 0),
        (1, cut, cut, 1, 1, 0),
        (2, 0, cut, 0, 0, cut),
        (2, cut, cut, 0, 1, cut),
        (3, 0, cut, 1, 0, cut),
        (3, cut, cut, 1, 1, cut),
    )

    def pack(key, units, layout, routes):
        own, send, table = dispatch(place, take(*units), layout, routes, capacity, tok_rows, wide)
        put(**{"own" + key: own, "table" + key: table})
        held["other" + key] = hop(send, CORE)

    def expert(key):
        mine, theirs = ffn(place, take("own" + key, "other" + key), w_gate, w_up, w_down)
        put(**{"own" + key: mine})
        held["back" + key] = hop(theirs, CORE)

    def mix(key, layout):
        return combine(place, [take("table" + key, "own" + key, "back" + key)], [layout], capacity)

    u0p = route(expert_ids.T, route_weights.T, tokens, wide)
    held.update(u0p=u0p, u2p=hop(u0p, FAR), u1p=hop(u0p, NEAR), u0p_y=hop(u0p, Y))
    held.update(u0_x=hop_x(tokens), u0_yx=hop_xy(tokens))

    def gather2():
        u2p = take("u2p")
        held.update(top2_x=hop_x(u2p[:cut]), low2_y=hop(u2p[cut:], Y), u3p=hop(u2p, NEAR))

    def gather2b():
        top_x, low_y, u2p = take("top2_x", "low2_y", "u2p")
        held.update(tops2=hop(rows(u2p[:cut], top_x), Y), lows2=hop_x(rows(u2p[cut:full], low_y[:cut])))
        held.update(u3_xy=hop(rows(top_x, low_y), NEAR))

    def gather1():
        held.update(u1_x=hop_x(take("u1p")[:full]))

    def gather1b():
        held.update(u1_ys=hop(rows(*take("u1p", "u1_x")), Y))

    def gather3():
        held.update(u3_yx=hop(rows(*take("tops2", "lows2")), NEAR))

    def pack0():
        layout = ((0, 0, full, 0, 0, 0), (1, 0, full, 1, 0, 0), (2, 0, full, 0, 1, 0), (3, 0, full, 1, 1, 0))
        pack("0", ("u0p", "u0_x", "u0p_y", "u0_yx"), layout, ((0, full), (2, full)))

    def pack2():
        pack("2", ("u2p", "top2_x", "low2_y", "tops2", "lows2"), halves, ((0, full), (2, cut)))

    def pack3():
        layout = (
            (0, 0, full, 0, 0, 0),
            (1, 0, cut, 1, 0, 0),
            (1, cut, cut, 0, 1, cut),
            (2, 0, cut, 0, 1, 0),
            (2, cut, cut, 1, 1, 0),
            (2, 2 * cut, cut, 1, 0, cut),
            (2, 3 * cut, cut, 1, 1, cut),
        )
        pack("3", ("u3p", "u3_xy", "u3_yx"), layout, ((0, full), (1, 2 * cut)))

    def pack1():
        layout = (
            (0, 0, full, 0, 0, 0),
            (1, 0, full, 1, 0, 0),
            (2, 0, full, 0, 1, 0),
            (2, full + wide, full, 1, 1, 0),
        )
        pack("1", ("u1p", "u1_x", "u1_ys"), layout, ((0, full), (2, full)))

    def mix_whole(key):
        def step():
            first_x = key in FIRST_X
            keep, send = mix(key, by_dx if first_x else by_dy)
            put(**{"keep" + key: keep})
            held["got" + key] = hop_x(send) if first_x else hop(send, Y)

        return step

    def sum_whole(key):
        def step():
            keep, got = take("keep" + key, "got" + key)
            both = add(keep, got)
            put(**{"keep" + key: both[:full]})
            held["got" + key] = hop(both[full:], Y) if key in FIRST_X else hop_x(both[full:])

        return step

    def end_whole(key):
        def step():
            end = add(*take("keep" + key, "got" + key))
            put(**{"end" + key: end if key == "0" else hop(end, FAR)})
            last[:] = [end]

        return step

    def expert31():
        names = ("own3", "own1", "other3", "other1")
        own3, own1, back3, back1 = ffn(place, take(*names), w_gate, w_up, w_down)
        put(own3=own3, own1=own1)
        held.update(back3=hop(back3, CORE), back1=hop(back1, CORE))

    def mix31():
        layouts = [
            tuple((number, at + p * full, count, dx, dy, row) for number, at, count, dx, dy, row in by_half)
            for p in (0, 1)
        ]
        names = ("table3", "own3", "back3", "table1", "own1", "back1")
        values = take(*names)
        keep_top, send_top, keep_low, send_low = combine(
            place, [values[:3], values[3:]], layouts, capacity
        )
        put(top=keep_top, low=keep_low)
        held.update(got_low=hop_x(send_low), got_top=hop(send_top, Y))

    def sum31():
        top, low, got_top, got_low = take("top", "low", "got_top", "got_low")
        top, low = add(top, got_top), add(low, got_low)
        put(top=rows(top[:cut], top[full : full + cut]), low=rows(low[:cut], low[full : full + cut]))
        held.update(got_top=hop_x(rows(top[cut:full], top[full + cut :])))
        held.update(got_low=hop(rows(low[cut:full], low[full + cut :]), Y))

    def out31():
        top, low, got_top, got_low = take("top", "low", "got_top", "got_low")
        top, low = add(top, got_top), add(low, got_low)
        put(end3=hop(rows(top[:cut], low[:cut]), NEAR | FAR), end1=hop(rows(top[cut:], low[cut:]), NEAR))
        last[:] = [top]

    steps = dict(
        gather2=gather2, gather2b=gather2b, gather1=gather1, gather1b=gather1b, gather3=gather3,
        pack0=pack0, pack1=pack1, pack2=pack2, pack3=pack3,
        expert0=lambda: expert("0"), expert2=lambda: expert("2"), expert31=expert31,
        mix0=mix_whole("0"), mix2=mix_whole("2"), mix31=mix31,
        sum0=sum_whole("0"), sum2=sum_whole("2"), sum31=sum31,
        out0=end_whole("0"), out2=end_whole("2"), out31=out31,
    )
    for step in ORDER:
        if step in steps:
            steps[step]()
        else:
            take(*step.split())
    total = sum(held["end" + key].astype(F32) for key in "0123")
    return total.astype(BF16)


def solution(mesh):
    in_specs = (
        P("wide", "narrow"),
        P("wide", None),
        P("wide", None),
        P("wide", "narrow", None),
        P("wide", "narrow", None),
        P("wide", "narrow", None),
    )
    out_specs = P("wide", "narrow")
    fits = mesh.shape["wide"] == 16 and mesh.shape["narrow"] == 2
    return jax.shard_map(
        local if fits else general, mesh=mesh, in_specs=in_specs, out_specs=out_specs, check_vma=False
    )
```

```python
import functools

import jax
import jax.numpy as jnp
from jax import lax
from jax.experimental import pallas as pl
from jax.experimental.pallas import tpu as pltpu
from jax.sharding import PartitionSpec as P

CORE, Y, NEAR, FAR = 1, 2, 4, 8
VMEM_BYTES = 20 << 20
ROUTE_FLOPS = 40_000_000_000
PACK_FLOPS = 10_000_000_000
MIX_FLOPS = 0
FIRST_X = ("2",)
ORDER = ["u1p", "gather12", "pack0", "gather2", "gather1", "expert0", "pack2", "gather3", "expert2", "mix0", "mix2", "pack1", "pack3", "expert31", "sum0", "mix3", "mix1", "sum2", "sum3", "out2", "sum1", "out3", "end2", "out1", "out0"]
F32, BF16 = jnp.float32, jnp.bfloat16


def general(tokens, expert_ids, route_weights, w_gate, w_up, w_down):
    tok_rows = expert_ids.shape[0]
    top_count = expert_ids.shape[1]
    local_experts = w_gate.shape[0]
    groups_wide = lax.axis_size("wide")
    experts_all = local_experts * groups_wide
    capacity = 7 * tok_rows * top_count // (6 * experts_all)
    slots_all = experts_all * capacity
    width = w_down.shape[2]
    flat_ids = expert_ids.reshape(-1)
    onehot = (flat_ids[:, None] == jnp.arange(experts_all, dtype=jnp.int32)[None, :]).astype(
        jnp.int32
    )
    running = jnp.cumsum(onehot, axis=0)
    slot_index = jnp.sum(running * onehot, axis=1) - 1
    destination = (flat_ids * capacity + slot_index).reshape(tok_rows, top_count)
    slot_table = (
        destination[:, :, None] == jnp.arange(slots_all, dtype=jnp.int32)[None, None, :]
    ).astype(jnp.float32)
    dispatch = jnp.sum(slot_table, axis=1).astype(jnp.bfloat16)
    whole = lax.all_gather(tokens, "narrow", axis=1, tiled=True)
    outgoing = jnp.einsum("ts,td->sd", dispatch, whole, preferred_element_type=jnp.float32).astype(
        jnp.bfloat16
    )
    received = lax.all_to_all(outgoing, "wide", split_axis=0, concat_axis=0, tiled=True)
    slot_rows = received.reshape(groups_wide, local_experts, capacity, width)
    gate_proj = jnp.einsum("secd,efd->secf", slot_rows, w_gate, preferred_element_type=jnp.float32)
    up_proj = jnp.einsum("secd,efd->secf", slot_rows, w_up, preferred_element_type=jnp.float32)
    hidden = (jax.nn.silu(gate_proj) * up_proj).astype(jnp.bfloat16)
    partial_value = jnp.einsum(
        "secf,efd->secd", hidden, w_down, preferred_element_type=jnp.float32
    ).astype(jnp.bfloat16)
    partial_value = partial_value.reshape(slots_all, width)
    summed = lax.psum_scatter(partial_value, "narrow", scatter_dimension=1, tiled=True).astype(
        jnp.float32
    )
    returned = lax.all_to_all(
        summed.astype(jnp.bfloat16), "wide", split_axis=0, concat_axis=0, tiled=True
    ).astype(summed.dtype)
    picked = returned[destination.reshape(-1)].reshape(tok_rows, top_count, -1)
    mixed = jnp.sum(route_weights.astype(jnp.float32)[:, :, None] * picked, axis=1)
    return mixed.astype(jnp.bfloat16)


def kernel_call(body, out_shape, n_in, flops, bytes_accessed, scratch=()):
    vmem = pl.BlockSpec(memory_space=pltpu.VMEM)
    return pl.pallas_call(
        body,
        out_shape=out_shape,
        in_specs=[pl.BlockSpec(memory_space=pltpu.SMEM)] + [vmem] * n_in,
        out_specs=jax.tree.map(lambda _: vmem, out_shape),
        scratch_shapes=list(scratch),
        compiler_params=pltpu.CompilerParams(vmem_limit_bytes=VMEM_BYTES),
        cost_estimate=pl.CostEstimate(flops=flops, bytes_accessed=bytes_accessed, transcendentals=0),
    )


def route_kernel(ids_ref, weights_ref, tokens_ref, out_ref):
    toks = tokens_ref.shape[0]
    experts = out_ref.shape[0] - toks
    total = jnp.zeros((experts, toks), F32)
    number = lax.broadcasted_iota(jnp.int32, (experts, toks), 0)
    weights = weights_ref[...].astype(F32)
    for k in range(ids_ref.shape[0]):
        total += jnp.where(number == ids_ref[k : k + 1, :], weights[k : k + 1, :], 0.0)
    out_ref[:toks] = tokens_ref[...]
    out_ref[toks:] = jnp.zeros((experts, out_ref.shape[1]), BF16)
    out_ref[toks:, :toks] = total.astype(BF16)


def route(ids, weights, tokens, experts):
    vmem = pl.BlockSpec(memory_space=pltpu.VMEM)
    return pl.pallas_call(
        route_kernel,
        out_shape=jax.ShapeDtypeStruct((tokens.shape[0] + experts, tokens.shape[1]), BF16),
        in_specs=[vmem] * 3,
        out_specs=vmem,
        cost_estimate=pl.CostEstimate(flops=ROUTE_FLOPS, bytes_accessed=1 << 16, transcendentals=0),
    )(ids, weights, tokens)


def routing_table(routes, toks, capacity, weighted):
    me = lax.axis_index("wide")
    before = lax.broadcasted_iota(jnp.int32, (toks, toks), 0) <= lax.broadcasted_iota(
        jnp.int32, (toks, toks), 1
    )
    number = lax.broadcasted_iota(jnp.int32, routes[0].shape, 0)
    weight = jnp.concatenate(
        [
            jnp.sum(jnp.where(number == expert, block, 0.0), axis=0, keepdims=True)
            for expert in (me, me ^ CORE)
            for block in routes
        ],
        axis=0,
    )
    chosen = weight > 0
    count = jnp.dot(
        jnp.where(chosen, 1.0, 0.0).astype(BF16),
        jnp.where(before, 1.0, 0.0).astype(BF16),
        preferred_element_type=F32,
    )
    slot = jnp.where(chosen, count.astype(jnp.int32) - 1, -1)
    tables = []
    for expert in (0, 1):
        first, second = slot[2 * expert : 2 * expert + 1], slot[2 * expert + 1 : 2 * expert + 2]
        second = jnp.where(second >= 0, second + capacity, -1)
        at = jnp.concatenate([first, second], axis=1)
        value = jnp.concatenate(
            [weight[2 * expert : 2 * expert + 1], weight[2 * expert + 1 : 2 * expert + 2]], axis=1
        )
        here = lax.broadcasted_iota(jnp.int32, (2 * capacity, 2 * toks), 0) == at
        tables.append(jnp.where(here, value if weighted else 1.0, 0.0))
    return jnp.concatenate(tables, axis=0).astype(BF16)


def dispatch_kernel(capacity, toks, layout, routes, place_ref, *refs):
    units, (own_ref, send_ref, routes_ref) = refs[:-3], refs[-3:]
    rows, half = 2 * capacity, own_ref.shape[1] // 2
    experts = routes_ref.shape[1]
    blocks = [units[number][row : row + experts, :toks].astype(F32) for number, row in routes]
    for i, block in enumerate(blocks):
        routes_ref[i] = block
    table = routing_table(blocks, toks, capacity, False)
    for dx in (0, 1):
        parts = []
        for number, at, count, column, dy, row in sorted(layout, key=lambda part: part[4:]):
            if column == dx:
                parts.append(units[number][at : at + count])
        out = jnp.dot(table, jnp.concatenate(parts, axis=0), preferred_element_type=F32).astype(BF16)
        own_ref[:, dx * half : (dx + 1) * half] = out[:rows]
        send_ref[:, dx * half : (dx + 1) * half] = out[rows:]


def dispatch(place, units, layout, routes, capacity, toks, experts, flops):
    half = units[0].shape[-1]
    shape = jax.ShapeDtypeStruct((2 * capacity, 2 * half), BF16)
    return kernel_call(
        functools.partial(dispatch_kernel, capacity, toks, layout, routes),
        (shape, shape, jax.ShapeDtypeStruct((2, experts, toks), F32)),
        len(units),
        flops,
        0,
    )(place, *units)


def ffn_kernel(count, place_ref, *refs):
    inputs, (gate_ref, up_ref, down_ref) = refs[:count], refs[count : count + 3]
    outputs, (rows_ref, hidden_ref) = refs[count + 3 : -2], refs[-2:]
    x = place_ref[1]
    n, half = inputs[0].shape[0], inputs[0].shape[1] // 2
    ff = gate_ref.shape[1]
    for i, ref in enumerate(inputs):
        rows_ref[i * n : (i + 1) * n] = ref[...]
    mine = pl.ds(pl.multiple_of(x * half, half), half)
    theirs = pl.ds(pl.multiple_of((1 - x) * half, half), half)
    step = 256
    nt = (((1,), (1,)), ((), ()))
    for low in range(0, ff, step):
        high = min(low + step, ff)

        def project(ref):
            return lax.dot_general(
                rows_ref[:, :half], ref[0, low:high, mine], nt, preferred_element_type=F32
            ) + lax.dot_general(
                rows_ref[:, half:], ref[0, low:high, theirs], nt, preferred_element_type=F32
            )

        gate = project(gate_ref)
        up = project(up_ref)
        hidden_ref[:, low:high] = (gate / (1.0 + jnp.exp(-gate)) * up).astype(BF16)
    for j, columns in enumerate((mine, theirs)):
        out = jnp.dot(hidden_ref[...], down_ref[0, :, columns], preferred_element_type=F32).astype(BF16)
        for i, ref in enumerate(outputs):
            ref[:, j * half : (j + 1) * half] = out[i * n : (i + 1) * n]


def ffn(place, inputs, w_gate, w_up, w_down):
    count = len(inputs)
    n, width = inputs[0].shape
    ff = w_gate.shape[1]
    return kernel_call(
        functools.partial(ffn_kernel, count),
        (jax.ShapeDtypeStruct((n, width), BF16),) * count,
        count + 3,
        count * n * width * ff,
        0,
        scratch=(pltpu.VMEM((count * n, width), BF16), pltpu.VMEM((count * n, ff), BF16)),
    )(place, *inputs, w_gate, w_up, w_down)


def combine_kernel(capacity, layouts, place_ref, *refs):
    count = len(layouts)
    inputs, outs = refs[: 3 * count], refs[3 * count :]
    half = inputs[1].shape[1] // 2
    toks = inputs[0].shape[2]
    for p, layout in enumerate(layouts):
        routes_ref, own_ref, other_ref = inputs[3 * p : 3 * p + 3]
        table = routing_table([routes_ref[0], routes_ref[1]], toks, capacity, True)
        for dx in (0, 1):
            columns = slice(dx * half, (dx + 1) * half)
            value = jnp.concatenate([own_ref[:, columns], other_ref[:, columns]], axis=0)
            out = lax.dot_general(
                table, value, (((0,), (0,)), ((), ())), preferred_element_type=F32
            ).astype(BF16)
            for number, at, count, column, dy, row in layout:
                if column == dx:
                    low = dy * toks + row
                    outs[number][at : at + count] = out[low : low + count]


def combine(place, pairs, layouts, capacity):
    toks, half = pairs[0][0].shape[2], pairs[0][1].shape[1] // 2
    parts = [part for layout in layouts for part in layout]
    rows = [0] * (1 + max(part[0] for part in parts))
    for part in parts:
        rows[part[0]] += part[2]
    return kernel_call(
        functools.partial(combine_kernel, capacity, layouts),
        tuple(jax.ShapeDtypeStruct((count, half), BF16) for count in rows),
        3 * len(pairs),
        MIX_FLOPS,
        0,
    )(place, *[array for pair in pairs for array in pair])


def local(tokens, expert_ids, route_weights, w_gate, w_up, w_down):
    wide = lax.axis_size("wide")
    tok_rows, top_count = expert_ids.shape
    capacity = 7 * tok_rows * top_count // (6 * wide)
    cut, full = tok_rows // 2, tok_rows
    me, x = lax.axis_index("wide"), lax.axis_index("narrow")
    place = jnp.stack([me, x]).astype(jnp.int32)

    def hop(value, bit):
        return lax.ppermute(value, "wide", [(i, i ^ bit) for i in range(wide)])

    def hop_x(value):
        return lax.ppermute(value, "narrow", [(0, 1), (1, 0)])

    def hop_xy(value):
        pairs = [(2 * i + j, 2 * (i ^ Y) + 1 - j) for i in range(wide) for j in (0, 1)]
        return lax.ppermute(value, ("wide", "narrow"), pairs)

    def add(a, b):
        return (a.astype(F32) + b.astype(F32)).astype(BF16)

    def rows(*parts):
        return jnp.concatenate(parts, axis=0)

    held, last = {}, []

    def take(*names):
        values = [held[name] for name in names]
        tied = lax.optimization_barrier(tuple(values + last))
        for name, value in zip(names, tied):
            held[name] = value
        last[:] = [tied[0]]
        return tied[0] if len(names) == 1 else tied[: len(names)]

    def put(**values):
        held.update(values)
        last[:] = [next(iter(values.values()))]

    halves = (
        (0, 0, full, 0, 0, 0),
        (1, 0, cut, 1, 0, 0),
        (2, 0, cut, 0, 1, cut),
        (3, 0, cut, 0, 1, 0),
        (3, cut, cut, 1, 1, 0),
        (4, 0, cut, 1, 0, cut),
        (4, cut, cut, 1, 1, cut),
    )
    by_dy = ((0, 0, full, 0, 0, 0), (0, full, full, 1, 0, 0), (1, 0, full, 0, 1, 0), (1, full, full, 1, 1, 0))
    by_dx = ((0, 0, full, 0, 0, 0), (0, full, full, 0, 1, 0), (1, 0, full, 1, 0, 0), (1, full, full, 1, 1, 0))
    by_half = (
        (0, 0, cut, 0, 0, 0),
        (0, cut, cut, 1, 0, 0),
        (1, 0, cut, 0, 1, 0),
        (1, cut, cut, 1, 1, 0),
        (2, 0, cut, 0, 0, cut),
        (2, cut, cut, 0, 1, cut),
        (3, 0, cut, 1, 0, cut),
        (3, cut, cut, 1, 1, cut),
    )

    def pack(key, units, layout, routes):
        own, send, table = dispatch(place, take(*units), layout, routes, capacity, tok_rows, wide, PACK_FLOPS if key == "0" else 0)
        put(**{"own" + key: own, "table" + key: table})
        held["other" + key] = hop(send, CORE)

    def expert(key):
        mine, theirs = ffn(place, take("own" + key, "other" + key), w_gate, w_up, w_down)
        put(**{"own" + key: mine})
        held["back" + key] = hop(theirs, CORE)

    def mix(key, layout):
        return combine(place, [take("table" + key, "own" + key, "back" + key)], [layout], capacity)

    u0p = route(expert_ids.T, route_weights.T, tokens, wide)
    held.update(u0p=u0p, u2p=hop(u0p, FAR), u1p=hop(u0p, NEAR), u0p_y=hop(u0p, Y))
    held.update(u0_x=hop_x(tokens), u0_yx=hop_xy(tokens))

    def gather12():
        u2p, u1p = take("u2p", "u1p")
        held.update(top_x=hop_x(rows(u2p[:cut], u1p[:cut])), low_y=hop(rows(u2p[cut:], u1p[cut:]), Y))
        held.update(u3p=hop(u2p, NEAR))

    def gather2():
        top_x, low_y, u2p = take("top_x", "low_y", "u2p")
        held.update(tops2=hop(rows(u2p[:cut], top_x[:cut]), Y))
        held.update(lows2=hop_x(rows(u2p[cut:full], low_y[:cut])))
        held.update(u3_xy=hop(rows(top_x[:cut], low_y[: cut + wide]), NEAR))

    def gather1():
        top_x, low_y, u1p = take("top_x", "low_y", "u1p")
        held.update(tops1=hop(rows(u1p[:cut], top_x[cut:]), Y))
        held.update(lows1=hop_x(rows(u1p[cut:full], low_y[cut + wide : full + wide])))

    def gather3():
        u3p, u3_xy = take("u3p", "u3_xy")
        held.update(tops3=hop(rows(u3p[:cut], u3_xy[:cut]), Y))
        held.update(lows3=hop_x(rows(u3p[cut:full], u3_xy[cut:full])))

    def pack0():
        layout = ((0, 0, full, 0, 0, 0), (1, 0, full, 1, 0, 0), (2, 0, full, 0, 1, 0), (3, 0, full, 1, 1, 0))
        pack("0", ("u0p", "u0_x", "u0p_y", "u0_yx"), layout, ((0, full), (2, full)))

    def pack2():
        pack("2", ("u2p", "top_x", "low_y", "tops2", "lows2"), halves, ((0, full), (2, cut)))

    def pack1():
        layout = ((0, 0, full, 0, 0, 0), (1, cut, cut, 1, 0, 0), (2, cut + wide, cut, 0, 1, cut)) + halves[3:]
        pack("1", ("u1p", "top_x", "low_y", "tops1", "lows1"), layout, ((0, full), (2, full + wide)))

    def pack3():
        layout = (
            (0, 0, full, 0, 0, 0),
            (1, 0, cut, 1, 0, 0),
            (1, cut, cut, 0, 1, cut),
            (2, 0, cut, 0, 1, 0),
            (2, cut, cut, 1, 1, 0),
            (3, 0, cut, 1, 0, cut),
            (3, cut, cut, 1, 1, cut),
        )
        pack("3", ("u3p", "u3_xy", "tops3", "lows3"), layout, ((0, full), (1, full)))

    def mix_whole(key):
        def step():
            first_x = key in FIRST_X
            keep, send = mix(key, by_dx if first_x else by_dy)
            put(**{"keep" + key: keep})
            held["got" + key] = hop_x(send) if first_x else hop(send, Y)

        return step

    def sum_whole(key):
        def step():
            keep, got = take("keep" + key, "got" + key)
            both = add(keep, got)
            put(**{"keep" + key: both[:full]})
            held["got" + key] = hop(both[full:], Y) if key in FIRST_X else hop_x(both[full:])

        return step

    def end_whole(key):
        def step():
            end = add(*take("keep" + key, "got" + key))
            put(**{"end" + key: end if key == "0" else hop(end, FAR)})
            last[:] = [end]

        return step

    def mix_halves(key):
        def step():
            keep_top, send_top, keep_low, send_low = mix(key, by_half)
            put(**{"top" + key: keep_top, "low" + key: keep_low})
            held.update({"got_low" + key: hop_x(send_low), "got_top" + key: hop(send_top, Y)})

        return step

    def sum_halves(key):
        def step():
            top, low, got_top, got_low = take("top" + key, "low" + key, "got_top" + key, "got_low" + key)
            top, low = add(top, got_top), add(low, got_low)
            put(**{"top" + key: top[:cut], "low" + key: low[:cut]})
            held.update({"got_top" + key: hop_x(top[cut:]), "got_low" + key: hop(low[cut:], Y)})

        return step

    def end_halves(key):
        def step():
            top, low, got_top, got_low = take("top" + key, "low" + key, "got_top" + key, "got_low" + key)
            end = rows(add(top, got_top), add(low, got_low))
            put(**{"end" + key: hop(end, NEAR | FAR if key == "3" else NEAR)})
            last[:] = [end]

        return step

    def expert_pair(a, b):
        def step():
            names = ("own" + a, "own" + b, "other" + a, "other" + b)
            own_a, own_b, back_a, back_b = ffn(place, take(*names), w_gate, w_up, w_down)
            put(**{"own" + a: own_a, "own" + b: own_b})
            held.update({"back" + a: hop(back_a, CORE), "back" + b: hop(back_b, CORE)})

        return step

    steps = dict(
        gather12=gather12, gather2=gather2, gather1=gather1, gather3=gather3,
        pack0=pack0, pack1=pack1, pack2=pack2, pack3=pack3,
        expert0=lambda: expert("0"), expert1=lambda: expert("1"), expert2=lambda: expert("2"),
        expert3=lambda: expert("3"), expert31=expert_pair("3", "1"), expert21=expert_pair("2", "1"),
        mix0=mix_whole("0"), mix2=mix_whole("2"), mix1=mix_halves("1"), mix3=mix_halves("3"),
        sum0=sum_whole("0"), sum2=sum_whole("2"), sum1=sum_halves("1"), sum3=sum_halves("3"),
        out0=end_whole("0"), out2=end_whole("2"), out1=end_halves("1"), out3=end_halves("3"),
    )
    for step in ORDER:
        if step in steps:
            steps[step]()
        else:
            take(*step.split())
    total = sum(held["end" + key].astype(F32) for key in "0123")
    return total.astype(BF16)


def solution(mesh):
    in_specs = (
        P("wide", "narrow"),
        P("wide", None),
        P("wide", None),
        P("wide", "narrow", None),
        P("wide", "narrow", None),
        P("wide", "narrow", None),
    )
    out_specs = P("wide", "narrow")
    fits = mesh.shape["wide"] == 16 and mesh.shape["narrow"] == 2
    return jax.shard_map(
        local if fits else general, mesh=mesh, in_specs=in_specs, out_specs=out_specs, check_vma=False
    )
```

```python
import functools

import jax
import jax.numpy as jnp
from jax import lax
from jax.experimental import pallas as pl
from jax.experimental.pallas import tpu as pltpu
from jax.sharding import PartitionSpec as P

CORE, Y, NEAR, FAR = 1, 2, 4, 8
VMEM_BYTES = 20 << 20
ROUTE_FLOPS = 40000000000
PACK_FLOPS = 3000000000
MIX_FLOPS = 0
REST_FLOPS = 0
FFN_WEIGHT = 1
FIRST_X = ("2",)
ORDER = ["u1p", "gather12", "pack0", "gather2", "gather1", "expert0", "pack2", "gather3", "expert2", "mix0", "mix2", "pack1", "pack3", "expert31", "sum0", "tops2", "tops3", "mix3", "mix1", "sum2", "sum3", "out2", "sum1", "out3", "end2", "out1", "out0"]
F32, BF16 = jnp.float32, jnp.bfloat16


def general(tokens, expert_ids, route_weights, w_gate, w_up, w_down):
    tok_rows = expert_ids.shape[0]
    top_count = expert_ids.shape[1]
    local_experts = w_gate.shape[0]
    groups_wide = lax.axis_size("wide")
    experts_all = local_experts * groups_wide
    capacity = 7 * tok_rows * top_count // (6 * experts_all)
    slots_all = experts_all * capacity
    width = w_down.shape[2]
    flat_ids = expert_ids.reshape(-1)
    onehot = (flat_ids[:, None] == jnp.arange(experts_all, dtype=jnp.int32)[None, :]).astype(
        jnp.int32
    )
    running = jnp.cumsum(onehot, axis=0)
    slot_index = jnp.sum(running * onehot, axis=1) - 1
    destination = (flat_ids * capacity + slot_index).reshape(tok_rows, top_count)
    slot_table = (
        destination[:, :, None] == jnp.arange(slots_all, dtype=jnp.int32)[None, None, :]
    ).astype(jnp.float32)
    dispatch = jnp.sum(slot_table, axis=1).astype(jnp.bfloat16)
    whole = lax.all_gather(tokens, "narrow", axis=1, tiled=True)
    outgoing = jnp.einsum("ts,td->sd", dispatch, whole, preferred_element_type=jnp.float32).astype(
        jnp.bfloat16
    )
    received = lax.all_to_all(outgoing, "wide", split_axis=0, concat_axis=0, tiled=True)
    slot_rows = received.reshape(groups_wide, local_experts, capacity, width)
    gate_proj = jnp.einsum("secd,efd->secf", slot_rows, w_gate, preferred_element_type=jnp.float32)
    up_proj = jnp.einsum("secd,efd->secf", slot_rows, w_up, preferred_element_type=jnp.float32)
    hidden = (jax.nn.silu(gate_proj) * up_proj).astype(jnp.bfloat16)
    partial_value = jnp.einsum(
        "secf,efd->secd", hidden, w_down, preferred_element_type=jnp.float32
    ).astype(jnp.bfloat16)
    partial_value = partial_value.reshape(slots_all, width)
    summed = lax.psum_scatter(partial_value, "narrow", scatter_dimension=1, tiled=True).astype(
        jnp.float32
    )
    returned = lax.all_to_all(
        summed.astype(jnp.bfloat16), "wide", split_axis=0, concat_axis=0, tiled=True
    ).astype(summed.dtype)
    picked = returned[destination.reshape(-1)].reshape(tok_rows, top_count, -1)
    mixed = jnp.sum(route_weights.astype(jnp.float32)[:, :, None] * picked, axis=1)
    return mixed.astype(jnp.bfloat16)


def kernel_call(body, out_shape, n_in, flops, bytes_accessed, scratch=()):
    vmem = pl.BlockSpec(memory_space=pltpu.VMEM)
    return pl.pallas_call(
        body,
        out_shape=out_shape,
        in_specs=[pl.BlockSpec(memory_space=pltpu.SMEM)] + [vmem] * n_in,
        out_specs=jax.tree.map(lambda _: vmem, out_shape),
        scratch_shapes=list(scratch),
        compiler_params=pltpu.CompilerParams(vmem_limit_bytes=VMEM_BYTES),
        cost_estimate=pl.CostEstimate(flops=flops, bytes_accessed=bytes_accessed, transcendentals=0),
    )


def route_kernel(ids_ref, weights_ref, tokens_ref, out_ref):
    toks = tokens_ref.shape[0]
    experts = out_ref.shape[0] - toks
    total = jnp.zeros((experts, toks), F32)
    number = lax.broadcasted_iota(jnp.int32, (experts, toks), 0)
    weights = weights_ref[...].astype(F32)
    for k in range(ids_ref.shape[0]):
        total += jnp.where(number == ids_ref[k : k + 1, :], weights[k : k + 1, :], 0.0)
    out_ref[:toks] = tokens_ref[...]
    out_ref[toks:] = jnp.zeros((experts, out_ref.shape[1]), BF16)
    out_ref[toks:, :toks] = total.astype(BF16)


def route(ids, weights, tokens, experts):
    vmem = pl.BlockSpec(memory_space=pltpu.VMEM)
    return pl.pallas_call(
        route_kernel,
        out_shape=jax.ShapeDtypeStruct((tokens.shape[0] + experts, tokens.shape[1]), BF16),
        in_specs=[vmem] * 3,
        out_specs=vmem,
        cost_estimate=pl.CostEstimate(flops=ROUTE_FLOPS, bytes_accessed=1 << 16, transcendentals=0),
    )(ids, weights, tokens)


def routing_table(routes, toks, capacity, weighted):
    me = lax.axis_index("wide")
    before = lax.broadcasted_iota(jnp.int32, (toks, toks), 0) <= lax.broadcasted_iota(
        jnp.int32, (toks, toks), 1
    )
    number = lax.broadcasted_iota(jnp.int32, routes[0].shape, 0)
    weight = jnp.concatenate(
        [
            jnp.sum(jnp.where(number == expert, block, 0.0), axis=0, keepdims=True)
            for expert in (me, me ^ CORE)
            for block in routes
        ],
        axis=0,
    )
    chosen = weight > 0
    count = jnp.dot(
        jnp.where(chosen, 1.0, 0.0).astype(BF16),
        jnp.where(before, 1.0, 0.0).astype(BF16),
        preferred_element_type=F32,
    )
    slot = jnp.where(chosen, count.astype(jnp.int32) - 1, -1)
    tables = []
    for expert in (0, 1):
        first, second = slot[2 * expert : 2 * expert + 1], slot[2 * expert + 1 : 2 * expert + 2]
        second = jnp.where(second >= 0, second + capacity, -1)
        at = jnp.concatenate([first, second], axis=1)
        value = jnp.concatenate(
            [weight[2 * expert : 2 * expert + 1], weight[2 * expert + 1 : 2 * expert + 2]], axis=1
        )
        here = lax.broadcasted_iota(jnp.int32, (2 * capacity, 2 * toks), 0) == at
        tables.append(jnp.where(here, value if weighted else 1.0, 0.0))
    return jnp.concatenate(tables, axis=0).astype(BF16)


def dispatch_kernel(capacity, toks, layout, routes, place_ref, *refs):
    units, (own_ref, send_ref, routes_ref) = refs[:-3], refs[-3:]
    rows, half = 2 * capacity, own_ref.shape[1] // 2
    experts = routes_ref.shape[1]
    blocks = [units[number][row : row + experts, :toks].astype(F32) for number, row in routes]
    for i, block in enumerate(blocks):
        routes_ref[i] = block
    table = routing_table(blocks, toks, capacity, False)
    for dx in (0, 1):
        parts = []
        for number, at, count, column, dy, row in sorted(layout, key=lambda part: part[4:]):
            if column == dx:
                parts.append(units[number][at : at + count])
        out = jnp.dot(table, jnp.concatenate(parts, axis=0), preferred_element_type=F32).astype(BF16)
        own_ref[:, dx * half : (dx + 1) * half] = out[:rows]
        send_ref[:, dx * half : (dx + 1) * half] = out[rows:]


def dispatch(place, units, layout, routes, capacity, toks, experts, flops):
    half = units[0].shape[-1]
    shape = jax.ShapeDtypeStruct((2 * capacity, 2 * half), BF16)
    return kernel_call(
        functools.partial(dispatch_kernel, capacity, toks, layout, routes),
        (shape, shape, jax.ShapeDtypeStruct((2, experts, toks), F32)),
        len(units),
        flops,
        0,
    )(place, *units)


def ffn_kernel(count, place_ref, *refs):
    inputs, (gate_ref, up_ref, down_ref) = refs[:count], refs[count : count + 3]
    outputs, (rows_ref, hidden_ref) = refs[count + 3 : -2], refs[-2:]
    x = place_ref[1]
    n, half = inputs[0].shape[0], inputs[0].shape[1] // 2
    ff = gate_ref.shape[1]
    for i, ref in enumerate(inputs):
        rows_ref[i * n : (i + 1) * n] = ref[...]
    mine = pl.ds(pl.multiple_of(x * half, half), half)
    theirs = pl.ds(pl.multiple_of((1 - x) * half, half), half)
    step = 256
    nt = (((1,), (1,)), ((), ()))
    for low in range(0, ff, step):
        high = min(low + step, ff)

        def project(ref):
            return lax.dot_general(
                rows_ref[:, :half], ref[0, low:high, mine], nt, preferred_element_type=F32
            ) + lax.dot_general(
                rows_ref[:, half:], ref[0, low:high, theirs], nt, preferred_element_type=F32
            )

        gate = project(gate_ref)
        up = project(up_ref)
        hidden_ref[:, low:high] = (gate / (1.0 + jnp.exp(-gate)) * up).astype(BF16)
    for j, columns in enumerate((mine, theirs)):
        out = jnp.dot(hidden_ref[...], down_ref[0, :, columns], preferred_element_type=F32).astype(BF16)
        for i, ref in enumerate(outputs):
            ref[:, j * half : (j + 1) * half] = out[i * n : (i + 1) * n]


def ffn(place, inputs, w_gate, w_up, w_down):
    count = len(inputs)
    n, width = inputs[0].shape
    ff = w_gate.shape[1]
    return kernel_call(
        functools.partial(ffn_kernel, count),
        (jax.ShapeDtypeStruct((n, width), BF16),) * count,
        count + 3,
        FFN_WEIGHT * count * n * width * ff,
        0,
        scratch=(pltpu.VMEM((count * n, width), BF16), pltpu.VMEM((count * n, ff), BF16)),
    )(place, *inputs, w_gate, w_up, w_down)


def combine_kernel(capacity, layouts, place_ref, *refs):
    count = len(layouts)
    inputs, outs = refs[: 3 * count], refs[3 * count :]
    half = inputs[1].shape[1] // 2
    toks = inputs[0].shape[2]
    for p, layout in enumerate(layouts):
        routes_ref, own_ref, other_ref = inputs[3 * p : 3 * p + 3]
        table = routing_table([routes_ref[0], routes_ref[1]], toks, capacity, True)
        for dx in (0, 1):
            columns = slice(dx * half, (dx + 1) * half)
            value = jnp.concatenate([own_ref[:, columns], other_ref[:, columns]], axis=0)
            out = lax.dot_general(
                table, value, (((0,), (0,)), ((), ())), preferred_element_type=F32
            ).astype(BF16)
            for number, at, count, column, dy, row in layout:
                if column == dx:
                    low = dy * toks + row
                    outs[number][at : at + count] = out[low : low + count]


def combine(place, pairs, layouts, capacity):
    toks, half = pairs[0][0].shape[2], pairs[0][1].shape[1] // 2
    parts = [part for layout in layouts for part in layout]
    rows = [0] * (1 + max(part[0] for part in parts))
    for part in parts:
        rows[part[0]] += part[2]
    return kernel_call(
        functools.partial(combine_kernel, capacity, layouts),
        tuple(jax.ShapeDtypeStruct((count, half), BF16) for count in rows),
        3 * len(pairs),
        MIX_FLOPS,
        0,
    )(place, *[array for pair in pairs for array in pair])


def local(tokens, expert_ids, route_weights, w_gate, w_up, w_down):
    wide = lax.axis_size("wide")
    tok_rows, top_count = expert_ids.shape
    capacity = 7 * tok_rows * top_count // (6 * wide)
    cut, full = tok_rows // 2, tok_rows
    me, x = lax.axis_index("wide"), lax.axis_index("narrow")
    place = jnp.stack([me, x]).astype(jnp.int32)

    def hop(value, bit):
        return lax.ppermute(value, "wide", [(i, i ^ bit) for i in range(wide)])

    def hop_x(value):
        return lax.ppermute(value, "narrow", [(0, 1), (1, 0)])

    def hop_xy(value):
        pairs = [(2 * i + j, 2 * (i ^ Y) + 1 - j) for i in range(wide) for j in (0, 1)]
        return lax.ppermute(value, ("wide", "narrow"), pairs)

    def add(a, b):
        return (a.astype(F32) + b.astype(F32)).astype(BF16)

    def rows(*parts):
        return jnp.concatenate(parts, axis=0)

    held, last = {}, []

    def take(*names):
        values = [held[name] for name in names]
        tied = lax.optimization_barrier(tuple(values + last))
        for name, value in zip(names, tied):
            held[name] = value
        last[:] = [tied[0]]
        return tied[0] if len(names) == 1 else tied[: len(names)]

    def put(**values):
        held.update(values)
        last[:] = [next(iter(values.values()))]

    halves = (
        (0, 0, full, 0, 0, 0),
        (1, 0, cut, 1, 0, 0),
        (2, 0, cut, 0, 1, cut),
        (3, 0, cut, 0, 1, 0),
        (3, cut, cut, 1, 1, 0),
        (4, 0, cut, 1, 0, cut),
        (4, cut, cut, 1, 1, cut),
    )
    by_dy = ((0, 0, full, 0, 0, 0), (0, full, full, 1, 0, 0), (1, 0, full, 0, 1, 0), (1, full, full, 1, 1, 0))
    by_dx = ((0, 0, full, 0, 0, 0), (0, full, full, 0, 1, 0), (1, 0, full, 1, 0, 0), (1, full, full, 1, 1, 0))
    by_half = (
        (0, 0, cut, 0, 0, 0),
        (0, cut, cut, 1, 0, 0),
        (1, 0, cut, 0, 1, 0),
        (1, cut, cut, 1, 1, 0),
        (2, 0, cut, 0, 0, cut),
        (2, cut, cut, 0, 1, cut),
        (3, 0, cut, 1, 0, cut),
        (3, cut, cut, 1, 1, cut),
    )

    def pack(key, units, layout, routes):
        own, send, table = dispatch(place, take(*units), layout, routes, capacity, tok_rows, wide, PACK_FLOPS if key == "0" else REST_FLOPS)
        put(**{"own" + key: own, "table" + key: table})
        held["other" + key] = hop(send, CORE)

    def expert(key):
        mine, theirs = ffn(place, take("own" + key, "other" + key), w_gate, w_up, w_down)
        put(**{"own" + key: mine})
        held["back" + key] = hop(theirs, CORE)

    def mix(key, layout):
        return combine(place, [take("table" + key, "own" + key, "back" + key)], [layout], capacity)

    u0p = route(expert_ids.T, route_weights.T, tokens, wide)
    held.update(u0p=u0p, u2p=hop(u0p, FAR), u1p=hop(u0p, NEAR), u0p_y=hop(u0p, Y))
    held.update(u0_x=hop_x(tokens), u0_yx=hop_xy(tokens))

    def gather12():
        u2p, u1p = take("u2p", "u1p")
        held.update(top_x=hop_x(rows(u2p[:cut], u1p[:cut])), low_y=hop(rows(u2p[cut:], u1p[cut:]), Y))
        held.update(u3p=hop(u2p, NEAR))

    def gather2():
        top_x, low_y, u2p = take("top_x", "low_y", "u2p")
        held.update(tops2=hop(rows(u2p[:cut], top_x[:cut]), Y))
        held.update(lows2=hop_x(rows(u2p[cut:full], low_y[:cut])))
        held.update(u3_xy=hop(rows(top_x[:cut], low_y[: cut + wide]), NEAR))

    def gather1():
        top_x, low_y, u1p = take("top_x", "low_y", "u1p")
        held.update(tops1=hop(rows(u1p[:cut], top_x[cut:]), Y))
        held.update(lows1=hop_x(rows(u1p[cut:full], low_y[cut + wide : full + wide])))

    def gather3():
        u3p, u3_xy = take("u3p", "u3_xy")
        held.update(tops3=hop(rows(u3p[:cut], u3_xy[:cut]), Y))
        held.update(lows3=hop_x(rows(u3p[cut:full], u3_xy[cut:full])))

    def pack0():
        layout = ((0, 0, full, 0, 0, 0), (1, 0, full, 1, 0, 0), (2, 0, full, 0, 1, 0), (3, 0, full, 1, 1, 0))
        pack("0", ("u0p", "u0_x", "u0p_y", "u0_yx"), layout, ((0, full), (2, full)))

    def pack2():
        pack("2", ("u2p", "top_x", "low_y", "tops2", "lows2"), halves, ((0, full), (2, cut)))

    def pack1():
        layout = ((0, 0, full, 0, 0, 0), (1, cut, cut, 1, 0, 0), (2, cut + wide, cut, 0, 1, cut)) + halves[3:]
        pack("1", ("u1p", "top_x", "low_y", "tops1", "lows1"), layout, ((0, full), (2, full + wide)))

    def pack3():
        layout = (
            (0, 0, full, 0, 0, 0),
            (1, 0, cut, 1, 0, 0),
            (1, cut, cut, 0, 1, cut),
            (2, 0, cut, 0, 1, 0),
            (2, cut, cut, 1, 1, 0),
            (3, 0, cut, 1, 0, cut),
            (3, cut, cut, 1, 1, cut),
        )
        pack("3", ("u3p", "u3_xy", "tops3", "lows3"), layout, ((0, full), (1, full)))

    def mix_whole(key):
        def step():
            first_x = key in FIRST_X
            keep, send = mix(key, by_dx if first_x else by_dy)
            put(**{"keep" + key: keep})
            held["got" + key] = hop_x(send) if first_x else hop(send, Y)

        return step

    def sum_whole(key):
        def step():
            keep, got = take("keep" + key, "got" + key)
            both = add(keep, got)
            put(**{"keep" + key: both[:full]})
            held["got" + key] = hop(both[full:], Y) if key in FIRST_X else hop_x(both[full:])

        return step

    def end_whole(key):
        def step():
            end = add(*take("keep" + key, "got" + key))
            put(**{"end" + key: end if key == "0" else hop(end, FAR)})
            last[:] = [end]

        return step

    def mix_halves(key):
        def step():
            keep_top, send_top, keep_low, send_low = mix(key, by_half)
            put(**{"top" + key: keep_top, "low" + key: keep_low})
            held.update({"got_low" + key: hop_x(send_low), "got_top" + key: hop(send_top, Y)})

        return step

    def sum_halves(key):
        def step():
            top, low, got_top, got_low = take("top" + key, "low" + key, "got_top" + key, "got_low" + key)
            top, low = add(top, got_top), add(low, got_low)
            put(**{"top" + key: top[:cut], "low" + key: low[:cut]})
            held.update({"got_top" + key: hop_x(top[cut:]), "got_low" + key: hop(low[cut:], Y)})

        return step

    def end_halves(key):
        def step():
            top, low, got_top, got_low = take("top" + key, "low" + key, "got_top" + key, "got_low" + key)
            end = rows(add(top, got_top), add(low, got_low))
            put(**{"end" + key: hop(end, NEAR | FAR if key == "3" else NEAR)})
            last[:] = [end]

        return step

    def expert_pair(a, b):
        def step():
            names = ("own" + a, "own" + b, "other" + a, "other" + b)
            own_a, own_b, back_a, back_b = ffn(place, take(*names), w_gate, w_up, w_down)
            put(**{"own" + a: own_a, "own" + b: own_b})
            held.update({"back" + a: hop(back_a, CORE), "back" + b: hop(back_b, CORE)})

        return step

    steps = dict(
        gather12=gather12, gather2=gather2, gather1=gather1, gather3=gather3,
        pack0=pack0, pack1=pack1, pack2=pack2, pack3=pack3,
        expert0=lambda: expert("0"), expert1=lambda: expert("1"), expert2=lambda: expert("2"),
        expert3=lambda: expert("3"), expert31=expert_pair("3", "1"), expert21=expert_pair("2", "1"),
        mix0=mix_whole("0"), mix2=mix_whole("2"), mix1=mix_halves("1"), mix3=mix_halves("3"),
        sum0=sum_whole("0"), sum2=sum_whole("2"), sum1=sum_halves("1"), sum3=sum_halves("3"),
        out0=end_whole("0"), out2=end_whole("2"), out1=end_halves("1"), out3=end_halves("3"),
    )
    for step in ORDER:
        if step in steps:
            steps[step]()
        else:
            take(*step.split())
    total = sum(held["end" + key].astype(F32) for key in "0123")
    return total.astype(BF16)


def solution(mesh):
    in_specs = (
        P("wide", "narrow"),
        P("wide", None),
        P("wide", None),
        P("wide", "narrow", None),
        P("wide", "narrow", None),
        P("wide", "narrow", None),
    )
    out_specs = P("wide", "narrow")
    fits = mesh.shape["wide"] == 16 and mesh.shape["narrow"] == 2
    return jax.shard_map(
        local if fits else general, mesh=mesh, in_specs=in_specs, out_specs=out_specs, check_vma=False
    )
```

```python
import functools

import jax
import jax.numpy as jnp
from jax import lax
from jax.experimental import pallas as pl
from jax.experimental.pallas import tpu as pltpu
from jax.sharding import PartitionSpec as P

CORE, Y, NEAR, FAR = 1, 2, 4, 8
VMEM_BYTES = 20 << 20
ROUTE_FLOPS = 40000000000
PACK_FLOPS = 3000000000
MIX_FLOPS = 0
REST_FLOPS = 0
FFN_WEIGHT = 1
FIRST_X = ("2",)
ORDER = ["u1p", "gather12", "pack0", "gather2", "gather1", "expert0", "pack2", "gather3", "expert2", "mix0", "mix2", "pack1", "pack3", "expert31", "sum0", "tops2", "tops3", "mix3", "mix1", "sum2", "sum3", "out2", "sum1", "out3", "end2", "out1", "out0"]
F32, BF16 = jnp.float32, jnp.bfloat16


def general(tokens, expert_ids, route_weights, w_gate, w_up, w_down):
    tok_rows = expert_ids.shape[0]
    top_count = expert_ids.shape[1]
    local_experts = w_gate.shape[0]
    groups_wide = lax.axis_size("wide")
    experts_all = local_experts * groups_wide
    capacity = 7 * tok_rows * top_count // (6 * experts_all)
    slots_all = experts_all * capacity
    width = w_down.shape[2]
    flat_ids = expert_ids.reshape(-1)
    onehot = (flat_ids[:, None] == jnp.arange(experts_all, dtype=jnp.int32)[None, :]).astype(
        jnp.int32
    )
    running = jnp.cumsum(onehot, axis=0)
    slot_index = jnp.sum(running * onehot, axis=1) - 1
    destination = (flat_ids * capacity + slot_index).reshape(tok_rows, top_count)
    slot_table = (
        destination[:, :, None] == jnp.arange(slots_all, dtype=jnp.int32)[None, None, :]
    ).astype(jnp.float32)
    dispatch = jnp.sum(slot_table, axis=1).astype(jnp.bfloat16)
    whole = lax.all_gather(tokens, "narrow", axis=1, tiled=True)
    outgoing = jnp.einsum("ts,td->sd", dispatch, whole, preferred_element_type=jnp.float32).astype(
        jnp.bfloat16
    )
    received = lax.all_to_all(outgoing, "wide", split_axis=0, concat_axis=0, tiled=True)
    slot_rows = received.reshape(groups_wide, local_experts, capacity, width)
    gate_proj = jnp.einsum("secd,efd->secf", slot_rows, w_gate, preferred_element_type=jnp.float32)
    up_proj = jnp.einsum("secd,efd->secf", slot_rows, w_up, preferred_element_type=jnp.float32)
    hidden = (jax.nn.silu(gate_proj) * up_proj).astype(jnp.bfloat16)
    partial_value = jnp.einsum(
        "secf,efd->secd", hidden, w_down, preferred_element_type=jnp.float32
    ).astype(jnp.bfloat16)
    partial_value = partial_value.reshape(slots_all, width)
    summed = lax.psum_scatter(partial_value, "narrow", scatter_dimension=1, tiled=True).astype(
        jnp.float32
    )
    returned = lax.all_to_all(
        summed.astype(jnp.bfloat16), "wide", split_axis=0, concat_axis=0, tiled=True
    ).astype(summed.dtype)
    picked = returned[destination.reshape(-1)].reshape(tok_rows, top_count, -1)
    mixed = jnp.sum(route_weights.astype(jnp.float32)[:, :, None] * picked, axis=1)
    return mixed.astype(jnp.bfloat16)


def kernel_call(body, out_shape, n_in, flops, bytes_accessed, scratch=()):
    vmem = pl.BlockSpec(memory_space=pltpu.VMEM)
    return pl.pallas_call(
        body,
        out_shape=out_shape,
        in_specs=[pl.BlockSpec(memory_space=pltpu.SMEM)] + [vmem] * n_in,
        out_specs=jax.tree.map(lambda _: vmem, out_shape),
        scratch_shapes=list(scratch),
        compiler_params=pltpu.CompilerParams(vmem_limit_bytes=VMEM_BYTES),
        cost_estimate=pl.CostEstimate(flops=flops, bytes_accessed=bytes_accessed, transcendentals=0),
    )


def route_kernel(ids_ref, weights_ref, tokens_ref, out_ref, own_ref):
    toks = tokens_ref.shape[0]
    experts = out_ref.shape[0] - toks
    total = jnp.zeros((experts, toks), F32)
    number = lax.broadcasted_iota(jnp.int32, (experts, toks), 0)
    weights = weights_ref[...].astype(F32)
    for k in range(ids_ref.shape[0]):
        total += jnp.where(number == ids_ref[k : k + 1, :], weights[k : k + 1, :], 0.0)
    out_ref[:toks] = tokens_ref[...]
    out_ref[toks:] = jnp.zeros((experts, out_ref.shape[1]), BF16)
    out_ref[toks:, :toks] = total.astype(BF16)
    own_ref[...] = out_ref[...]


def route(ids, weights, tokens, experts):
    vmem = pl.BlockSpec(memory_space=pltpu.VMEM)
    return pl.pallas_call(
        route_kernel,
        out_shape=(jax.ShapeDtypeStruct((tokens.shape[0] + experts, tokens.shape[1]), BF16),) * 2,
        in_specs=[vmem] * 3,
        out_specs=(vmem, vmem),
        cost_estimate=pl.CostEstimate(flops=ROUTE_FLOPS, bytes_accessed=1 << 16, transcendentals=0),
    )(ids, weights, tokens)


def routing_table(routes, toks, capacity, weighted):
    me = lax.axis_index("wide")
    before = lax.broadcasted_iota(jnp.int32, (toks, toks), 0) <= lax.broadcasted_iota(
        jnp.int32, (toks, toks), 1
    )
    number = lax.broadcasted_iota(jnp.int32, routes[0].shape, 0)
    weight = jnp.concatenate(
        [
            jnp.sum(jnp.where(number == expert, block, 0.0), axis=0, keepdims=True)
            for expert in (me, me ^ CORE)
            for block in routes
        ],
        axis=0,
    )
    chosen = weight > 0
    count = jnp.dot(
        jnp.where(chosen, 1.0, 0.0).astype(BF16),
        jnp.where(before, 1.0, 0.0).astype(BF16),
        preferred_element_type=F32,
    )
    slot = jnp.where(chosen, count.astype(jnp.int32) - 1, -1)
    tables = []
    for expert in (0, 1):
        first, second = slot[2 * expert : 2 * expert + 1], slot[2 * expert + 1 : 2 * expert + 2]
        second = jnp.where(second >= 0, second + capacity, -1)
        at = jnp.concatenate([first, second], axis=1)
        value = jnp.concatenate(
            [weight[2 * expert : 2 * expert + 1], weight[2 * expert + 1 : 2 * expert + 2]], axis=1
        )
        here = lax.broadcasted_iota(jnp.int32, (2 * capacity, 2 * toks), 0) == at
        tables.append(jnp.where(here, value if weighted else 1.0, 0.0))
    return jnp.concatenate(tables, axis=0).astype(BF16)


def dispatch_kernel(capacity, toks, layout, routes, place_ref, *refs):
    units, (own_ref, send_ref, routes_ref) = refs[:-3], refs[-3:]
    rows, half = 2 * capacity, own_ref.shape[1] // 2
    experts = routes_ref.shape[1]
    blocks = [units[number][row : row + experts, :toks].astype(F32) for number, row in routes]
    for i, block in enumerate(blocks):
        routes_ref[i] = block
    table = routing_table(blocks, toks, capacity, False)
    for dx in (0, 1):
        parts = []
        for number, at, count, column, dy, row in sorted(layout, key=lambda part: part[4:]):
            if column == dx:
                parts.append(units[number][at : at + count])
        out = jnp.dot(table, jnp.concatenate(parts, axis=0), preferred_element_type=F32).astype(BF16)
        own_ref[:, dx * half : (dx + 1) * half] = out[:rows]
        send_ref[:, dx * half : (dx + 1) * half] = out[rows:]


def dispatch(place, units, layout, routes, capacity, toks, experts, flops):
    half = units[0].shape[-1]
    shape = jax.ShapeDtypeStruct((2 * capacity, 2 * half), BF16)
    return kernel_call(
        functools.partial(dispatch_kernel, capacity, toks, layout, routes),
        (shape, shape, jax.ShapeDtypeStruct((2, experts, toks), F32)),
        len(units),
        flops,
        0,
    )(place, *units)


def ffn_kernel(count, place_ref, *refs):
    inputs, (gate_ref, up_ref, down_ref) = refs[:count], refs[count : count + 3]
    outputs, (rows_ref, hidden_ref) = refs[count + 3 : -2], refs[-2:]
    x = place_ref[1]
    n, half = inputs[0].shape[0], inputs[0].shape[1] // 2
    ff = gate_ref.shape[1]
    for i, ref in enumerate(inputs):
        rows_ref[i * n : (i + 1) * n] = ref[...]
    mine = pl.ds(pl.multiple_of(x * half, half), half)
    theirs = pl.ds(pl.multiple_of((1 - x) * half, half), half)
    step = 256
    nt = (((1,), (1,)), ((), ()))
    for low in range(0, ff, step):
        high = min(low + step, ff)

        def project(ref):
            return lax.dot_general(
                rows_ref[:, :half], ref[0, low:high, mine], nt, preferred_element_type=F32
            ) + lax.dot_general(
                rows_ref[:, half:], ref[0, low:high, theirs], nt, preferred_element_type=F32
            )

        gate = project(gate_ref)
        up = project(up_ref)
        hidden_ref[:, low:high] = (gate / (1.0 + jnp.exp(-gate)) * up).astype(BF16)
    for j, columns in enumerate((mine, theirs)):
        out = jnp.dot(hidden_ref[...], down_ref[0, :, columns], preferred_element_type=F32).astype(BF16)
        for i, ref in enumerate(outputs):
            ref[:, j * half : (j + 1) * half] = out[i * n : (i + 1) * n]


def ffn(place, inputs, w_gate, w_up, w_down):
    count = len(inputs)
    n, width = inputs[0].shape
    ff = w_gate.shape[1]
    return kernel_call(
        functools.partial(ffn_kernel, count),
        (jax.ShapeDtypeStruct((n, width), BF16),) * count,
        count + 3,
        FFN_WEIGHT * count * n * width * ff,
        0,
        scratch=(pltpu.VMEM((count * n, width), BF16), pltpu.VMEM((count * n, ff), BF16)),
    )(place, *inputs, w_gate, w_up, w_down)


def combine_kernel(capacity, layouts, place_ref, *refs):
    count = len(layouts)
    inputs, outs = refs[: 3 * count], refs[3 * count :]
    half = inputs[1].shape[1] // 2
    toks = inputs[0].shape[2]
    for p, layout in enumerate(layouts):
        routes_ref, own_ref, other_ref = inputs[3 * p : 3 * p + 3]
        table = routing_table([routes_ref[0], routes_ref[1]], toks, capacity, True)
        for dx in (0, 1):
            columns = slice(dx * half, (dx + 1) * half)
            value = jnp.concatenate([own_ref[:, columns], other_ref[:, columns]], axis=0)
            out = lax.dot_general(
                table, value, (((0,), (0,)), ((), ())), preferred_element_type=F32
            ).astype(BF16)
            for number, at, count, column, dy, row in layout:
                if column == dx:
                    low = dy * toks + row
                    outs[number][at : at + count] = out[low : low + count]


def combine(place, pairs, layouts, capacity):
    toks, half = pairs[0][0].shape[2], pairs[0][1].shape[1] // 2
    parts = [part for layout in layouts for part in layout]
    rows = [0] * (1 + max(part[0] for part in parts))
    for part in parts:
        rows[part[0]] += part[2]
    return kernel_call(
        functools.partial(combine_kernel, capacity, layouts),
        tuple(jax.ShapeDtypeStruct((count, half), BF16) for count in rows),
        3 * len(pairs),
        MIX_FLOPS,
        0,
    )(place, *[array for pair in pairs for array in pair])


def local(tokens, expert_ids, route_weights, w_gate, w_up, w_down):
    wide = lax.axis_size("wide")
    tok_rows, top_count = expert_ids.shape
    capacity = 7 * tok_rows * top_count // (6 * wide)
    cut, full = tok_rows // 2, tok_rows
    me, x = lax.axis_index("wide"), lax.axis_index("narrow")
    place = jnp.stack([me, x]).astype(jnp.int32)

    def hop(value, bit):
        return lax.ppermute(value, "wide", [(i, i ^ bit) for i in range(wide)])

    def hop_x(value):
        return lax.ppermute(value, "narrow", [(0, 1), (1, 0)])

    def hop_xy(value):
        pairs = [(2 * i + j, 2 * (i ^ Y) + 1 - j) for i in range(wide) for j in (0, 1)]
        return lax.ppermute(value, ("wide", "narrow"), pairs)

    def add(a, b):
        return (a.astype(F32) + b.astype(F32)).astype(BF16)

    def rows(*parts):
        return jnp.concatenate(parts, axis=0)

    held, last = {}, []

    def take(*names):
        values = [held[name] for name in names]
        tied = lax.optimization_barrier(tuple(values + last))
        for name, value in zip(names, tied):
            held[name] = value
        last[:] = [tied[0]]
        return tied[0] if len(names) == 1 else tied[: len(names)]

    def put(**values):
        held.update(values)
        last[:] = [next(iter(values.values()))]

    halves = (
        (0, 0, full, 0, 0, 0),
        (1, 0, cut, 1, 0, 0),
        (2, 0, cut, 0, 1, cut),
        (3, 0, cut, 0, 1, 0),
        (3, cut, cut, 1, 1, 0),
        (4, 0, cut, 1, 0, cut),
        (4, cut, cut, 1, 1, cut),
    )
    by_dy = ((0, 0, full, 0, 0, 0), (0, full, full, 1, 0, 0), (1, 0, full, 0, 1, 0), (1, full, full, 1, 1, 0))
    by_dx = ((0, 0, full, 0, 0, 0), (0, full, full, 0, 1, 0), (1, 0, full, 1, 0, 0), (1, full, full, 1, 1, 0))
    by_half = (
        (0, 0, cut, 0, 0, 0),
        (0, cut, cut, 1, 0, 0),
        (1, 0, cut, 0, 1, 0),
        (1, cut, cut, 1, 1, 0),
        (2, 0, cut, 0, 0, cut),
        (2, cut, cut, 0, 1, cut),
        (3, 0, cut, 1, 0, cut),
        (3, cut, cut, 1, 1, cut),
    )

    def pack(key, units, layout, routes):
        own, send, table = dispatch(place, take(*units), layout, routes, capacity, tok_rows, wide, PACK_FLOPS if key == "0" else REST_FLOPS)
        put(**{"own" + key: own, "table" + key: table})
        held["other" + key] = hop(send, CORE)

    def expert(key):
        mine, theirs = ffn(place, take("own" + key, "other" + key), w_gate, w_up, w_down)
        put(**{"own" + key: mine})
        held["back" + key] = hop(theirs, CORE)

    def mix(key, layout):
        return combine(place, [take("table" + key, "own" + key, "back" + key)], [layout], capacity)

    u0p, u0_own = route(expert_ids.T, route_weights.T, tokens, wide)
    held.update(u0p=u0_own, u2p=hop(u0p, FAR), u1p=hop(u0p, NEAR), u0p_y=hop(u0p, Y))
    held.update(u0_x=hop_x(tokens), u0_yx=hop_xy(tokens))

    def gather12():
        u2p, u1p = take("u2p", "u1p")
        held.update(top_x=hop_x(rows(u2p[:cut], u1p[:cut])), low_y=hop(rows(u2p[cut:], u1p[cut:]), Y))
        held.update(u3p=hop(u2p, NEAR))

    def gather2():
        top_x, low_y, u2p = take("top_x", "low_y", "u2p")
        held.update(tops2=hop(rows(u2p[:cut], top_x[:cut]), Y))
        held.update(lows2=hop_x(rows(u2p[cut:full], low_y[:cut])))
        held.update(u3_xy=hop(rows(top_x[:cut], low_y[: cut + wide]), NEAR))

    def gather1():
        top_x, low_y, u1p = take("top_x", "low_y", "u1p")
        held.update(tops1=hop(rows(u1p[:cut], top_x[cut:]), Y))
        held.update(lows1=hop_x(rows(u1p[cut:full], low_y[cut + wide : full + wide])))

    def gather3():
        u3p, u3_xy = take("u3p", "u3_xy")
        held.update(tops3=hop(rows(u3p[:cut], u3_xy[:cut]), Y))
        held.update(lows3=hop_x(rows(u3p[cut:full], u3_xy[cut:full])))

    def pack0():
        layout = ((0, 0, full, 0, 0, 0), (1, 0, full, 1, 0, 0), (2, 0, full, 0, 1, 0), (3, 0, full, 1, 1, 0))
        pack("0", ("u0p", "u0_x", "u0p_y", "u0_yx"), layout, ((0, full), (2, full)))

    def pack2():
        pack("2", ("u2p", "top_x", "low_y", "tops2", "lows2"), halves, ((0, full), (2, cut)))

    def pack1():
        layout = ((0, 0, full, 0, 0, 0), (1, cut, cut, 1, 0, 0), (2, cut + wide, cut, 0, 1, cut)) + halves[3:]
        pack("1", ("u1p", "top_x", "low_y", "tops1", "lows1"), layout, ((0, full), (2, full + wide)))

    def pack3():
        layout = (
            (0, 0, full, 0, 0, 0),
            (1, 0, cut, 1, 0, 0),
            (1, cut, cut, 0, 1, cut),
            (2, 0, cut, 0, 1, 0),
            (2, cut, cut, 1, 1, 0),
            (3, 0, cut, 1, 0, cut),
            (3, cut, cut, 1, 1, cut),
        )
        pack("3", ("u3p", "u3_xy", "tops3", "lows3"), layout, ((0, full), (1, full)))

    def mix_whole(key):
        def step():
            first_x = key in FIRST_X
            keep, send = mix(key, by_dx if first_x else by_dy)
            put(**{"keep" + key: keep})
            held["got" + key] = hop_x(send) if first_x else hop(send, Y)

        return step

    def sum_whole(key):
        def step():
            keep, got = take("keep" + key, "got" + key)
            both = add(keep, got)
            put(**{"keep" + key: both[:full]})
            held["got" + key] = hop(both[full:], Y) if key in FIRST_X else hop_x(both[full:])

        return step

    def end_whole(key):
        def step():
            end = add(*take("keep" + key, "got" + key))
            put(**{"end" + key: end if key == "0" else hop(end, FAR)})
            last[:] = [end]

        return step

    def mix_halves(key):
        def step():
            keep_top, send_top, keep_low, send_low = mix(key, by_half)
            put(**{"top" + key: keep_top, "low" + key: keep_low})
            held.update({"got_low" + key: hop_x(send_low), "got_top" + key: hop(send_top, Y)})

        return step

    def sum_halves(key):
        def step():
            top, low, got_top, got_low = take("top" + key, "low" + key, "got_top" + key, "got_low" + key)
            top, low = add(top, got_top), add(low, got_low)
            put(**{"top" + key: top[:cut], "low" + key: low[:cut]})
            held.update({"got_top" + key: hop_x(top[cut:]), "got_low" + key: hop(low[cut:], Y)})

        return step

    def end_halves(key):
        def step():
            top, low, got_top, got_low = take("top" + key, "low" + key, "got_top" + key, "got_low" + key)
            end = rows(add(top, got_top), add(low, got_low))
            put(**{"end" + key: hop(end, NEAR | FAR if key == "3" else NEAR)})
            last[:] = [end]

        return step

    def expert_pair(a, b):
        def step():
            names = ("own" + a, "own" + b, "other" + a, "other" + b)
            own_a, own_b, back_a, back_b = ffn(place, take(*names), w_gate, w_up, w_down)
            put(**{"own" + a: own_a, "own" + b: own_b})
            held.update({"back" + a: hop(back_a, CORE), "back" + b: hop(back_b, CORE)})

        return step

    steps = dict(
        gather12=gather12, gather2=gather2, gather1=gather1, gather3=gather3,
        pack0=pack0, pack1=pack1, pack2=pack2, pack3=pack3,
        expert0=lambda: expert("0"), expert1=lambda: expert("1"), expert2=lambda: expert("2"),
        expert3=lambda: expert("3"), expert31=expert_pair("3", "1"), expert21=expert_pair("2", "1"),
        mix0=mix_whole("0"), mix2=mix_whole("2"), mix1=mix_halves("1"), mix3=mix_halves("3"),
        sum0=sum_whole("0"), sum2=sum_whole("2"), sum1=sum_halves("1"), sum3=sum_halves("3"),
        out0=end_whole("0"), out2=end_whole("2"), out1=end_halves("1"), out3=end_halves("3"),
    )
    for step in ORDER:
        if step in steps:
            steps[step]()
        else:
            take(*step.split())
    total = sum(held["end" + key].astype(F32) for key in "0123")
    return total.astype(BF16)


def solution(mesh):
    in_specs = (
        P("wide", "narrow"),
        P("wide", None),
        P("wide", None),
        P("wide", "narrow", None),
        P("wide", "narrow", None),
        P("wide", "narrow", None),
    )
    out_specs = P("wide", "narrow")
    fits = mesh.shape["wide"] == 16 and mesh.shape["narrow"] == 2
    return jax.shard_map(
        local if fits else general, mesh=mesh, in_specs=in_specs, out_specs=out_specs, check_vma=False
    )
```
